512 devices in a mesh: gx: 64 (over y, z_lo, core), gy: 8 (over z_hi, x).
Axes of the slice: x: 4, y: 4, z: 16 (z_hi: 2, z_lo: 8; z = z_hi * 8 + z_lo), core: 2. Of those that a mesh axis runs over, the one named last changes fastest.
Arguments:
- grid_field: bfloat16 [2, 1024, 256, 512], P(None, 'gx', 'gy'), may hold values from -6 to 6
- spectral_weight: bfloat16 [128, 2, 512, 512], P('gx', None, None, 'gy'), may hold values from -0.1875 to 0.1875
- skip_weight: bfloat16 [512, 512], replicated, may hold values from -0.25 to 0.25
- inner_weight: bfloat16 [1024, 512], replicated, may hold values from -0.25 to 0.25
- outer_weight: bfloat16 [1024, 512], replicated, may hold values from -0.1875 to 0.1875
Outputs:
- layer_out: bfloat16 [2, 1024, 256, 512], P(None, 'gx', 'gy')
The draws below stay inside these ranges and needn't reach their ends.
All inputs are finite; a program needn't handle non-finite values.
Results may differ from the reference program's by a relative error of at most 0.0093.
Values may be sent and summed in bfloat16 or wider, within the bound.
A program may use at most 64 MiB of HBM per device.

```python
import math
import jax
import jax.numpy as jnp
from jax import lax

WIDTH = 512
HIDDEN_SIZE = 1024
KX = 16
KY = 8
BATCH = 2
CX = 16
MODES = 128
NX = 1024
NY = 256


def shard_levels(rng, extent, cuts, least, largest):
    loudness, own = 1.0, jax.random.fold_in(rng, 6)
    for axis_at, parts in cuts:
        heights = jnp.exp(jax.random.uniform(jax.random.fold_in(own, axis_at), (parts,), jnp.float32, least / len(cuts), largest / len(cuts)))
        loudness = loudness * jnp.repeat(heights, extent[axis_at] // parts).reshape([-1 if axis == axis_at else 1 for axis in range(len(extent))])
    return loudness


def bell_draw(key, shape, spread, limit, shards=(), kind=jnp.bfloat16):
    entries = jax.random.normal(key, shape, jnp.float32) * spread
    if len(shards) > 0:
        entries = shard_levels(key, shape, shards, -0.22, 0.18) * entries
    return jnp.clip(entries, min=-limit, max=limit).astype(kind)


def setup_inputs(seed: int = 0) -> dict:
    arg_keys = jax.random.split(jax.random.key(seed), 6)
    grid_field = bell_draw(arg_keys[0], (BATCH, NX, NY, WIDTH), 1.0, 6.0, ((1, 64), (2, 8)))
    spectral_weight = bell_draw(arg_keys[1], (MODES, 2, WIDTH, WIDTH), (2 * WIDTH) ** -0.5, 0.1875, ((0, 64), (3, 8)))
    skip_weight = bell_draw(arg_keys[2], (WIDTH, WIDTH), WIDTH ** -0.5, 0.25)
    inner_weight = bell_draw(arg_keys[3], (HIDDEN_SIZE, WIDTH), WIDTH ** -0.5, 0.25)
    outer_weight = bell_draw(arg_keys[4], (HIDDEN_SIZE, WIDTH), HIDDEN_SIZE ** -0.5, 0.1875)
    return dict(grid_field=grid_field, spectral_weight=spectral_weight, skip_weight=skip_weight, inner_weight=inner_weight, outer_weight=outer_weight)


def phase_table(row_ids, col_ids, total_rows, total_cols):
    x_modes = jnp.arange(KX, dtype=jnp.int32)
    y_modes = jnp.arange(KY, dtype=jnp.int32)
    x_phase = (x_modes[:, None] * row_ids[None, :] % total_rows).astype(jnp.float32) / total_rows
    y_phase = (y_modes[:, None] * col_ids[None, :] % total_cols).astype(jnp.float32) / total_cols
    angles = (x_phase[:, None, :, None] + y_phase[None, :, None, :]) * (2.0 * math.pi)
    angles = angles.reshape(KX * KY, row_ids.shape[0] * col_ids.shape[0])
    return jnp.concatenate([jnp.cos(angles), -jnp.sin(angles)], axis=0).astype(jnp.bfloat16)

def reference(grid_field, spectral_weight, skip_weight, inner_weight, outer_weight):
    col_ids = jnp.arange(NY, dtype=jnp.int32)
    block_count = NX // CX

    def forward(running, block_id):
        row_ids = block_id * CX + jnp.arange(CX, dtype=jnp.int32)
        basis = phase_table(row_ids, col_ids, NX, NY).astype(jnp.float32)
        piece = lax.dynamic_slice_in_dim(grid_field, (block_id * CX).astype(jnp.int32), CX, 1)
        piece = piece.reshape(BATCH, CX * NY, WIDTH).astype(jnp.float32)
        return (running + jnp.einsum('kn,bnc->kbc', basis, piece), None)
    summed, _ = lax.scan(forward, jnp.zeros((2 * MODES, BATCH, WIDTH), jnp.float32), jnp.arange(block_count, dtype=jnp.int32))
    spectrum = (summed * (1.0 / math.sqrt(NX * NY))).astype(jnp.bfloat16).reshape(2, MODES, BATCH, WIDTH)
    spec_re = spectrum[0].astype(jnp.float32)
    spec_im = spectrum[1].astype(jnp.float32)
    weight_re = spectral_weight[:, 0].astype(jnp.float32)
    weight_im = spectral_weight[:, 1].astype(jnp.float32)
    mixed_re = jnp.einsum('mbc,mcd->mbd', spec_re, weight_re) - jnp.einsum('mbc,mcd->mbd', spec_im, weight_im)
    mixed_im = jnp.einsum('mbc,mcd->mbd', spec_re, weight_im) + jnp.einsum('mbc,mcd->mbd', spec_im, weight_re)
    mixed_modes = jnp.stack([mixed_re, mixed_im]).astype(jnp.bfloat16).reshape(2 * MODES, BATCH, WIDTH)
    mixed_float = mixed_modes.astype(jnp.float32)
    skip_float = skip_weight.astype(jnp.float32)
    inner_float = inner_weight.astype(jnp.float32)
    outer_float = outer_weight.astype(jnp.float32)

    def backward(block_id):
        row_ids = block_id * CX + jnp.arange(CX, dtype=jnp.int32)
        basis = phase_table(row_ids, col_ids, NX, NY).astype(jnp.float32)
        piece = lax.dynamic_slice_in_dim(grid_field, (block_id * CX).astype(jnp.int32), CX, 1)
        piece = piece.reshape(BATCH, CX * NY, WIDTH).astype(jnp.float32)
        spectral = jnp.einsum('kn,kbc->bnc', basis, mixed_float) * (1.0 / math.sqrt(MODES))
        skip_term = jnp.einsum('bnc,cd->bnd', piece, skip_float)
        active = jax.nn.gelu(spectral + skip_term).astype(jnp.bfloat16)
        hidden = jax.nn.gelu(jnp.einsum('bnc,hc->bnh', active.astype(jnp.float32), inner_float)).astype(jnp.bfloat16)
        feed_forward = jnp.einsum('bnh,hc->bnc', hidden.astype(jnp.float32), outer_float)
        return (active.astype(jnp.float32) + feed_forward).astype(jnp.bfloat16)
    blocks_out = lax.map(backward, jnp.arange(block_count, dtype=jnp.int32))
    blocks_out = blocks_out.reshape(block_count, BATCH, CX, NY, WIDTH)
    return blocks_out.transpose(1, 0, 2, 3, 4).reshape(BATCH, NX, NY, WIDTH)
```

```python
import math

import numpy as np
import jax
import jax.numpy as jnp
from jax import lax
from jax.experimental import pallas as pl
from jax.experimental.pallas import tpu as pltpu
from jax.sharding import PartitionSpec as P

MESH = pl.DeviceIdType.MESH
F32 = jnp.float32
BF16 = jnp.bfloat16
KX = 16
KY = 8
ROWS = 16
COLS = 32
CELLS = ROWS * COLS
NX = 1024
NY = 256
WIDTH = 512
HIDDEN = 1024
SPECTRUM_SCALE = 1.0 / math.sqrt(NX * NY)
FIELD_SCALE = 1.0 / math.sqrt(KX * KY)


def local_tables():
    core, y, j, z = np.meshgrid(np.arange(2), np.arange(4), np.arange(2), np.arange(8), indexing="ij")
    kx = (y * 4 + z // 2).reshape(2, 4, 16, 1, 1)
    ky = ((z % 2) * 4 + core * 2 + j).reshape(2, 4, 16, 1, 1)
    dx = np.arange(ROWS).reshape(1, 1, 1, ROWS, 1)
    dy = np.arange(COLS).reshape(1, 1, 1, 1, COLS)
    angle = 2.0 * np.pi * (kx * dx / NX + ky * dy / NY)
    angle = angle.reshape(2, 4, 16, CELLS)
    return np.stack([np.cos(angle), np.sin(angle)], axis=2).astype(np.float32)


def gelu(v):
    a = math.sqrt(2.0 / math.pi)
    t = jnp.tanh(v * (a + (a * 0.044715) * (v * v)))
    h = 0.5 * v
    return h + h * t


def body(
    field_hbm, weight_hbm, skip_hbm, inner_hbm, outer_hbm, table_hbm, out_ref,
    field, wv, skip, inner, outer, table,
    basis, basis_t, inner_t, pre,
    csend, crecv, own, xsend, xrecv, zsend, zrecv, ssend, srecv, gsend, grecv, blocks, spread,
    load_sem, cs_sem, cr_sem, xs_sem, xr_sem, zs_sem, zr_sem, ss_sem, sr_sem,
    gs_sem, gr_sem, bs_sem, br_sem, as_sem, ar_sem,
):
    gx, gy = lax.axis_index("gx"), lax.axis_index("gy")
    my, mzl, mc = gx // 16, (gx // 2) % 8, gx % 2
    mzh, mx = gy // 4, gy % 4
    mz = mzh * 8 + mzl

    def at(y, z, c, x):
        return (y * 16 + (z % 8) * 2 + c, (z // 8) * 4 + x)

    sibling = at(my, mz, 1 - mc, mx)
    plane = []
    for d in range(1, 16):
        x, y = (mx + d % 4) % 4, (my + d // 4) % 4
        plane.append((d, x, y, at(y, mz, mc, x)))
    column = []
    for d in (8, 7, 9, 6, 10, 5, 11, 4, 12, 3, 13, 2, 14, 1, 15):
        z = (mz + d) % 16
        column.append((d, z, at(my, z, mc, mx)))
    row = []
    for d in (2, 1, 3):
        x = (mx + d) % 4
        row.append((d, x, at(my, mz, mc, x)))

    barrier = pltpu.get_barrier_semaphore()
    for peer in [p[-1] for p in column] + [p[-1] for p in plane] + [sibling]:
        pl.semaphore_signal(barrier, inc=1, device_id=peer, device_id_type=MESH)

    loads = []

    def load(src, dst):
        copy = pltpu.make_async_copy(src, dst, load_sem.at[len(loads)])
        copy.start()
        loads.append(copy)
        return copy

    table_in = load(table_hbm, table)
    field_in = [load(field_hbm.at[b], field.at[b]) for b in range(2)]
    weight_in = [
        load(weight_hbm.at[j, q], wv.at[q, pl.ds(j * 64, 64)]) for j in range(2) for q in range(2)
    ]
    skip_in = load(skip_hbm, skip)
    inner_in = load(inner_hbm, inner)
    outer_in = load(outer_hbm, outer)

    index = lax.broadcasted_iota(jnp.int32, (16, 128), 0)
    table_in.wait()

    def make_basis(core):
        for y in range(4):
            j, z = index // 8, index % 8
            kx = y * 4 + z // 2
            ky = (z % 2) * 4 + core * 2 + j
            x_phase = ((kx * (gx * ROWS)) % NX).astype(F32) * (1.0 / NX)
            y_phase = ((ky * (gy * COLS)) % NY).astype(F32) * (1.0 / NY)
            phase = x_phase + y_phase
            phase = jnp.where(phase >= 1.0, phase - 1.0, phase)
            phase = jnp.where(phase >= 0.5, phase - 1.0, phase)
            c0 = jnp.cos(phase * (2.0 * math.pi))
            s0 = jnp.sin(phase * (2.0 * math.pi))
            for t in range(4):
                lanes = pl.ds(t * 128, 128)
                cd = table[core, y, 0, :, lanes]
                sd = table[core, y, 1, :, lanes]
                basis[core, y, 0, :, lanes] = (c0 * cd - s0 * sd).astype(BF16)
                basis[core, y, 1, :, lanes] = (-(s0 * cd + c0 * sd)).astype(BF16)

    def forward(core, b):
        rows = basis[core].reshape(128, CELLS)
        return jnp.dot(rows, field[b], preferred_element_type=F32)

    make_basis(1 - mc)
    core_copies = []
    for b in range(2):
        field_in[b].wait()
        part = forward(1 - mc, b)
        csend[b] = part.astype(BF16)
        if b == 0:
            pl.semaphore_wait(barrier, 31)
        copy = pltpu.make_async_remote_copy(
            src_ref=csend.at[b], dst_ref=crecv.at[b], send_sem=cs_sem.at[b], recv_sem=cr_sem.at[b],
            device_id=sibling, device_id_type=MESH,
        )
        copy.start()
        core_copies.append(copy)
    make_basis(mc)
    for b in range(2):
        own[b] = forward(mc, b)

    plane_copies = []
    for b in range(2):
        core_copies[b].wait_recv()
        for x in range(4):
            lanes = pl.ds(x * 128, 128)
            both = own[b, :, lanes] + crecv[b, :, lanes].astype(F32)
            own[b, :, lanes] = both
            xsend[b, x] = both.astype(BF16).reshape(4, 32, 128)
        for d, x, y, peer in plane:
            copy = pltpu.make_async_remote_copy(
                src_ref=xsend.at[b, x, y], dst_ref=xrecv.at[b, d], send_sem=xs_sem.at[b, d],
                recv_sem=xr_sem.at[b, d], device_id=peer, device_id_type=MESH,
            )
            copy.start()
            plane_copies.append(copy)

    skip_in.wait()
    for b in range(2):
        pre[b] = jnp.dot(field[b], skip[...], preferred_element_type=F32)

    for b in range(2):
        total = xsend[b, mx, my].astype(F32)
        for d in range(1, 16):
            plane_copies[b * 15 + d - 1].wait_recv()
            total = total + xrecv[b, d].astype(F32)
        for ri in range(2):
            for j in range(2):
                zsend[pl.ds(b * 4 + ri * 2 + j, 8, stride=8), :] = total[ri * 16 + j * 8 : ri * 16 + j * 8 + 8]

    column_copies = []
    for d, z, peer in column:
        copy = pltpu.make_async_remote_copy(
            src_ref=zsend.at[pl.ds(pl.multiple_of((z % 8) * 8, 8), 8)], dst_ref=zrecv.at[d],
            send_sem=zs_sem.at[d], recv_sem=zr_sem.at[d], device_id=peer, device_id_type=MESH,
        )
        copy.start()
        column_copies.append(copy)

    for core in range(2):
        for y in range(4):
            for ri in range(2):
                pass
    for t in range(4):
        cells = pl.ds(t * 128, 128)
        basis_t[cells, :] = basis[:, :, :, :, cells].reshape(256, 128).T
    inner_in.wait()
    for t in range(8):
        units = pl.ds(t * 128, 128)
        inner_t[:, units] = inner[units, :].T
    for copy in core_copies + plane_copies:
        copy.wait_send()

    total = zsend[pl.ds(pl.multiple_of(mzl * 8, 8), 8), :]
    for copy, (d, _, _) in zip(column_copies, column):
        copy.wait_recv()
        total = total + zrecv[d]
    spectrum = (total * SPECTRUM_SCALE).astype(BF16).astype(F32)

    ssend[...] = spectrum
    row_copies = []
    for d, x, peer in row:
        copy = pltpu.make_async_remote_copy(
            src_ref=ssend, dst_ref=srecv.at[mx], send_sem=ss_sem.at[d], recv_sem=sr_sem.at[d],
            device_id=peer, device_id_type=MESH,
        )
        copy.start()
        row_copies.append(copy)
    srecv[mx] = spectrum
    for copy in weight_in:
        copy.wait()
    for copy in column_copies:
        copy.wait_send()
    for copy in row_copies:
        copy.wait_recv()
    modes = jnp.concatenate([srecv[x] for x in range(4)], axis=1).astype(BF16)
    nt = (((1,), (1,)), ((), ()))
    by_re = lax.dot_general(modes, wv[0], nt, preferred_element_type=F32)
    by_im = lax.dot_general(modes, wv[1], nt, preferred_element_type=F32)
    low = lax.broadcasted_iota(jnp.int32, (1, 128), 1) < 64

    def pick(v, b, ri):
        k = b * 4 + ri * 2
        return jnp.where(low, v[k : k + 1], v[k + 1 : k + 2])

    mixed = []
    for b in range(2):
        mixed.append(pick(by_re, b, 0) - pick(by_im, b, 1))
        mixed.append(pick(by_im, b, 0) + pick(by_re, b, 1))
    mixed = jnp.concatenate(mixed + mixed, axis=0).astype(BF16).astype(F32)

    gsend[...] = mixed
    back_copies = []
    for d, z, peer in column:
        copy = pltpu.make_async_remote_copy(
            src_ref=gsend, dst_ref=grecv.at[pl.ds(pl.multiple_of(mz * 8, 8), 8)],
            send_sem=gs_sem.at[d], recv_sem=gr_sem.at[d], device_id=peer, device_id_type=MESH,
        )
        copy.start()
        back_copies.append(copy)
    grecv[pl.ds(pl.multiple_of(mz * 8, 8), 8), :] = mixed
    outer_in.wait()
    for copy in row_copies:
        copy.wait_send()
    for copy in back_copies:
        copy.wait_recv()

    low8 = lax.broadcasted_iota(jnp.int32, (8, 128), 1) < 64
    for b in range(2):
        for ri in range(2):
            k = b * 2 + ri
            first = grecv[pl.ds(k, 8, stride=8), :]
            second = grecv[pl.ds(64 + k, 8, stride=8), :]
            j0 = jnp.where(low8, first, pltpu.roll(second, 64, 1))
            j1 = jnp.where(low8, pltpu.roll(first, 64, 1), second)
            blocks[mx, my, b, ri] = jnp.concatenate([j0, j1], axis=0).astype(BF16)

    spread_copies = []
    for d, x, y, peer in plane:
        copy = pltpu.make_async_remote_copy(
            src_ref=blocks.at[mx, my], dst_ref=blocks.at[mx, my], send_sem=bs_sem.at[d],
            recv_sem=br_sem.at[d], device_id=peer, device_id_type=MESH,
        )
        copy.start()
        spread_copies.append(copy)
    for copy in back_copies:
        copy.wait_send()

    low16 = lax.broadcasted_iota(jnp.int32, (16, 128), 1) < 64
    pair_copies = []
    for dy in (0, 1, 3, 2):
        for dx in range(4):
            d = dy * 4 + dx
            if d:
                spread_copies[d - 1].wait_recv()
        y = (my + 4 - dy) % 4
        for b in range(2):
            for ri in range(2):
                for h in range(2):
                    even = blocks[2 * h, y, b, ri].astype(F32)
                    odd = blocks[2 * h + 1, y, b, ri].astype(F32)
                    near = jnp.where(low16, even, pltpu.roll(odd, 64, 1))
                    far = jnp.where(low16, pltpu.roll(even, 64, 1), odd)
                    spread[mc, y, b, ri, :, pl.ds(h * 128, 128)] = near.astype(BF16)
                    spread[mc, y, b, ri, :, pl.ds(256 + h * 128, 128)] = far.astype(BF16)
        copy = pltpu.make_async_remote_copy(
            src_ref=spread.at[mc, y], dst_ref=spread.at[mc, y], send_sem=as_sem.at[dy],
            recv_sem=ar_sem.at[dy], device_id=sibling, device_id_type=MESH,
        )
        copy.start()
        pair_copies.append(copy)
    for copy in spread_copies:
        copy.wait_send()
    for copy in pair_copies:
        copy.wait_recv()

    for b in range(2):
        modes = spread[:, :, b].reshape(256, WIDTH)
        for h in range(2):
            cells = pl.ds(h * 256, 256)
            spectral = jnp.dot(basis_t[cells, :], modes, preferred_element_type=F32)
            active = gelu(spectral * FIELD_SCALE + pre[b, cells, :]).astype(BF16)
            hidden = jnp.dot(active, inner_t[...], preferred_element_type=F32)
            hidden = gelu(hidden).astype(BF16)
            added = jnp.dot(hidden, outer[...], preferred_element_type=F32)
            out_ref[b, cells, :] = (active.astype(F32) + added).astype(BF16)
    for copy in pair_copies:
        copy.wait_send()


def local(grid_field, spectral_weight, skip_weight, inner_weight, outer_weight):
    table = jnp.asarray(local_tables())
    field = grid_field.reshape(2, CELLS, WIDTH)
    weight = jnp.swapaxes(spectral_weight, 2, 3)
    dma = pltpu.SemaphoreType.DMA
    out = pl.pallas_call(
        body,
        out_shape=jax.ShapeDtypeStruct((2, CELLS, WIDTH), BF16),
        in_specs=[pl.BlockSpec(memory_space=pl.ANY)] * 6,
        out_specs=pl.BlockSpec(memory_space=pltpu.VMEM),
        scratch_shapes=[
            pltpu.VMEM((2, CELLS, WIDTH), BF16),
            pltpu.VMEM((2, 128, WIDTH), BF16),
            pltpu.VMEM((WIDTH, WIDTH), BF16),
            pltpu.VMEM((HIDDEN, WIDTH), BF16),
            pltpu.VMEM((HIDDEN, WIDTH), BF16),
            pltpu.VMEM((2, 4, 2, 16, CELLS), F32),
            pltpu.VMEM((2, 4, 2, 16, CELLS), BF16),
            pltpu.VMEM((CELLS, 256), BF16),
            pltpu.VMEM((WIDTH, HIDDEN), BF16),
            pltpu.VMEM((2, CELLS, WIDTH), F32),
            pltpu.VMEM((2, 128, WIDTH), BF16),
            pltpu.VMEM((2, 128, WIDTH), BF16),
            pltpu.VMEM((2, 128, WIDTH), F32),
            pltpu.VMEM((2, 4, 4, 32, 128), BF16),
            pltpu.VMEM((2, 16, 32, 128), BF16),
            pltpu.VMEM((64, 128), F32),
            pltpu.VMEM((16, 8, 128), F32),
            pltpu.VMEM((8, 128), F32),
            pltpu.VMEM((4, 8, 128), F32),
            pltpu.VMEM((8, 128), F32),
            pltpu.VMEM((128, 128), F32),
            pltpu.VMEM((4, 4, 2, 2, 16, 128), BF16),
            pltpu.VMEM((2, 4, 2, 2, 16, WIDTH), BF16),
            dma((10,)),
            dma((2,)), dma((2,)),
            dma((2, 16)), dma((2, 16)),
            dma((16,)), dma((16,)),
            dma((4,)), dma((4,)),
            dma((16,)), dma((16,)),
            dma((16,)), dma((16,)),
            dma((4,)), dma((4,)),
        ],
        compiler_params=pltpu.CompilerParams(
            collective_id=0, has_side_effects=True, vmem_limit_bytes=40 << 20
        ),
        cost_estimate=pl.CostEstimate(flops=3_400_000_000, bytes_accessed=7 << 20, transcendentals=1_600_000),
    )(field, weight, skip_weight, inner_weight, outer_weight, table)
    return out.reshape(grid_field.shape)


def solution(mesh):
    in_specs = (P(None, "gx", "gy", None), P("gx", None, None, "gy"), P(), P(), P())
    out_specs = P(None, "gx", "gy", None)
    return jax.shard_map(local, mesh=mesh, in_specs=in_specs, out_specs=out_specs, check_vma=False)
```

```python
import math

import numpy as np
import jax
import jax.numpy as jnp
from jax import lax
from jax.experimental import pallas as pl
from jax.experimental.pallas import tpu as pltpu
from jax.sharding import PartitionSpec as P

MESH = pl.DeviceIdType.MESH
F32 = jnp.float32
BF16 = jnp.bfloat16
KX = 16
KY = 8
ROWS = 16
COLS = 32
CELLS = ROWS * COLS
NX = 1024
NY = 256
WIDTH = 512
HIDDEN = 1024
SPECTRUM_SCALE = 1.0 / math.sqrt(NX * NY)
FIELD_SCALE = 1.0 / math.sqrt(KX * KY)


def local_tables():
    core, y, j, z = np.meshgrid(np.arange(2), np.arange(4), np.arange(2), np.arange(8), indexing="ij")
    kx = (y * 4 + z // 2).reshape(2, 4, 16, 1, 1)
    ky = ((z % 2) * 4 + core * 2 + j).reshape(2, 4, 16, 1, 1)
    dx = np.arange(ROWS).reshape(1, 1, 1, ROWS, 1)
    dy = np.arange(COLS).reshape(1, 1, 1, 1, COLS)
    angle = 2.0 * np.pi * (kx * dx / NX + ky * dy / NY)
    angle = angle.reshape(2, 4, 16, CELLS)
    return np.stack([np.cos(angle), np.sin(angle)], axis=2).astype(np.float32)


def gelu(v):
    a = math.sqrt(2.0 / math.pi)
    t = jnp.tanh(v * (a + (a * 0.044715) * (v * v)))
    h = 0.5 * v
    return h + h * t


def body(
    field_hbm, weight_hbm, skip_hbm, inner_hbm, outer_hbm, table_hbm, out_hbm,
    field, wv, skip, inner, outer, table,
    basis, basis_t, inner_t, pre,
    csend, crecv, own, xsend, xrecv, zsend, zrecv, ssend, srecv, gsend, grecv, blocks, spread, result,
    load_sem, cs_sem, cr_sem, xs_sem, xr_sem, zs_sem, zr_sem, ss_sem, sr_sem,
    gs_sem, gr_sem, bs_sem, br_sem, as_sem, ar_sem, store_sem, across_ready, near_ready, far_ready,
):
    gx, gy = lax.axis_index("gx"), lax.axis_index("gy")
    my, mzl, mc = gx // 16, (gx // 2) % 8, gx % 2
    mzh, mx = gy // 4, gy % 4
    mz = mzh * 8 + mzl

    def at(y, z, c, x):
        return (y * 16 + (z % 8) * 2 + c, (z // 8) * 4 + x)

    sibling = at(my, mz, 1 - mc, mx)
    plane = []
    for d in range(1, 16):
        x, y = (mx + d % 4) % 4, (my + d // 4) % 4
        plane.append((d, x, y, at(y, mz, mc, x)))
    column = []
    for d in (8, 7, 9, 6, 10, 5, 11, 4, 12, 3, 13, 2, 14, 1, 15):
        z = (mz + d) % 16
        column.append((d, z, at(my, z, mc, mx)))
    row = []
    for d in (2, 1, 3):
        x = (mx + d) % 4
        row.append((d, x, at(my, mz, mc, x)))

    def signal(semaphore, peers):
        for peer in peers:
            pl.semaphore_signal(semaphore, inc=1, device_id=peer, device_id_type=MESH)

    barrier = pltpu.get_barrier_semaphore()
    across = [at((my + d) % 4, mz, mc, mx) for d in (2, 1, 3)]
    along = {d: at(my, (mz + d) % 16, mc, mx) for d in (1, 2, 4, 12, 14, 15)}
    near = [sibling] + [p[-1] for p in row] + across + [along[d] for d in (2, 14, 1, 15)]
    signal(barrier, near)

    loads = []

    def load(src, dst):
        copy = pltpu.make_async_copy(src, dst, load_sem.at[len(loads)])
        copy.start()
        loads.append(copy)
        return copy

    first_in = load(table_hbm.at[1 - mc], table.at[1 - mc])
    field_in = [load(field_hbm.at[b], field.at[b]) for b in range(2)]
    second_in = load(table_hbm.at[mc], table.at[mc])

    index = lax.broadcasted_iota(jnp.int32, (16, 128), 0)
    lane = lax.broadcasted_iota(jnp.int32, (16, 128), 1)
    kx = (lane % 4) * 4 + (index % 8) // 2
    ky = (index % 2) * 4 + jnp.where(lane < 4, 1 - mc, mc) * 2 + index // 8
    x_phase = ((kx * (gx * ROWS)) % NX).astype(F32) * (1.0 / NX)
    y_phase = ((ky * (gy * COLS)) % NY).astype(F32) * (1.0 / NY)
    phase = x_phase + y_phase
    phase = jnp.where(phase >= 1.0, phase - 1.0, phase)
    phase = jnp.where(phase >= 0.5, phase - 1.0, phase)
    cos0 = jnp.cos(phase * (2.0 * math.pi))
    sin0 = jnp.sin(phase * (2.0 * math.pi))

    def make_basis(core, column0):
        for y in range(4):
            at_lane = slice(column0 + y, column0 + y + 1)
            c0 = jnp.broadcast_to(cos0[:, at_lane], (16, 128))
            s0 = jnp.broadcast_to(sin0[:, at_lane], (16, 128))
            for t in range(4):
                lanes = pl.ds(t * 128, 128)
                cd = table[core, y, 0, :, lanes]
                sd = table[core, y, 1, :, lanes]
                basis[core, y, 0, :, lanes] = (c0 * cd - s0 * sd).astype(BF16)
                basis[core, y, 1, :, lanes] = (-(s0 * cd + c0 * sd)).astype(BF16)

    def forward(core, b):
        rows = basis[core].reshape(128, CELLS)
        return jnp.dot(rows, field[b], preferred_element_type=F32)

    first_in.wait()
    make_basis(1 - mc, 0)
    core_copies = []
    for b in range(2):
        field_in[b].wait()
        part = forward(1 - mc, b)
        csend[b] = part.astype(BF16)
        if b == 0:
            pl.semaphore_wait(barrier, 11)
            signal(across_ready, across)
            signal(near_ready, [along[2], along[14]])
        copy = pltpu.make_async_remote_copy(
            src_ref=csend.at[b], dst_ref=crecv.at[b], send_sem=cs_sem.at[b], recv_sem=cr_sem.at[b],
            device_id=sibling, device_id_type=MESH,
        )
        copy.start()
        core_copies.append(copy)
    weight_in = [
        load(weight_hbm.at[j, q], wv.at[q, pl.ds(j * 64, 64)]) for j in range(2) for q in range(2)
    ]
    skip_in = load(skip_hbm, skip)
    inner_in = load(inner_hbm, inner)
    outer_in = load(outer_hbm, outer)
    second_in.wait()
    make_basis(mc, 4)
    for b in range(2):
        own[b] = forward(mc, b)

    plane_copies = []
    for b in range(2):
        core_copies[b].wait_recv()
        for x in range(4):
            lanes = pl.ds(x * 128, 128)
            both = own[b, :, lanes] + crecv[b, :, lanes].astype(F32)
            own[b, :, lanes] = both
            xsend[b, x] = both.astype(BF16).reshape(4, 32, 128)
        if b == 0:
            pl.semaphore_wait(across_ready, 3)
        for d, x, y, peer in plane:
            copy = pltpu.make_async_remote_copy(
                src_ref=xsend.at[b, x, y], dst_ref=xrecv.at[b, d], send_sem=xs_sem.at[b, d],
                recv_sem=xr_sem.at[b, d], device_id=peer, device_id_type=MESH,
            )
            copy.start()
            plane_copies.append(copy)

    pl.semaphore_wait(near_ready, 2)
    signal(far_ready, [along[4], along[12]])
    skip_in.wait()
    for b in range(2):
        pre[b] = jnp.dot(field[b], skip[...], preferred_element_type=F32)

    for b in range(2):
        total = xsend[b, mx, my].astype(F32)
        for d in range(1, 16):
            plane_copies[b * 15 + d - 1].wait_recv()
            total = total + xrecv[b, d].astype(F32)
        for ri in range(2):
            for j in range(2):
                zsend[pl.ds(b * 4 + ri * 2 + j, 8, stride=8), :] = total[ri * 16 + j * 8 : ri * 16 + j * 8 + 8]

    pl.semaphore_wait(far_ready, 2)
    column_copies = []
    for d, z, peer in column:
        copy = pltpu.make_async_remote_copy(
            src_ref=zsend.at[pl.ds(pl.multiple_of((z % 8) * 8, 8), 8)], dst_ref=zrecv.at[d],
            send_sem=zs_sem.at[d], recv_sem=zr_sem.at[d], device_id=peer, device_id_type=MESH,
        )
        copy.start()
        column_copies.append(copy)

    for t in range(4):
        cells = pl.ds(t * 128, 128)
        basis_t[cells, :] = basis[:, :, :, :, cells].reshape(256, 128).T
    inner_in.wait()
    for t in range(8):
        units = pl.ds(t * 128, 128)
        inner_t[:, units] = inner[units, :].T
    for copy in core_copies + plane_copies:
        copy.wait_send()

    total = zsend[pl.ds(pl.multiple_of(mzl * 8, 8), 8), :]
    for copy, (d, _, _) in zip(column_copies, column):
        copy.wait_recv()
        total = total + zrecv[d]
    spectrum = (total * SPECTRUM_SCALE).astype(BF16).astype(F32)

    ssend[...] = spectrum
    row_copies = []
    for d, x, peer in row:
        copy = pltpu.make_async_remote_copy(
            src_ref=ssend, dst_ref=srecv.at[mx], send_sem=ss_sem.at[d], recv_sem=sr_sem.at[d],
            device_id=peer, device_id_type=MESH,
        )
        copy.start()
        row_copies.append(copy)
    srecv[mx] = spectrum
    for copy in weight_in:
        copy.wait()
    for copy in column_copies:
        copy.wait_send()
    for copy in row_copies:
        copy.wait_recv()
    modes = jnp.concatenate([srecv[x] for x in range(4)], axis=1).astype(BF16)
    nt = (((1,), (1,)), ((), ()))
    by_re = lax.dot_general(modes, wv[0], nt, preferred_element_type=F32)
    by_im = lax.dot_general(modes, wv[1], nt, preferred_element_type=F32)
    low = lax.broadcasted_iota(jnp.int32, (1, 128), 1) < 64

    def pick(v, b, ri):
        k = b * 4 + ri * 2
        return jnp.where(low, v[k : k + 1], v[k + 1 : k + 2])

    mixed = []
    for b in range(2):
        mixed.append(pick(by_re, b, 0) - pick(by_im, b, 1))
        mixed.append(pick(by_im, b, 0) + pick(by_re, b, 1))
    mixed = jnp.concatenate(mixed + mixed, axis=0).astype(BF16).astype(F32)

    gsend[...] = mixed
    back_copies = []
    for d, z, peer in column:
        copy = pltpu.make_async_remote_copy(
            src_ref=gsend, dst_ref=grecv.at[pl.ds(pl.multiple_of(mz * 8, 8), 8)],
            send_sem=gs_sem.at[d], recv_sem=gr_sem.at[d], device_id=peer, device_id_type=MESH,
        )
        copy.start()
        back_copies.append(copy)
    grecv[pl.ds(pl.multiple_of(mz * 8, 8), 8), :] = mixed
    outer_in.wait()
    for copy in row_copies:
        copy.wait_send()
    for copy in back_copies:
        copy.wait_recv()

    low8 = lax.broadcasted_iota(jnp.int32, (8, 128), 1) < 64
    for b in range(2):
        for ri in range(2):
            k = b * 2 + ri
            first = grecv[pl.ds(k, 8, stride=8), :]
            second = grecv[pl.ds(64 + k, 8, stride=8), :]
            j0 = jnp.where(low8, first, pltpu.roll(second, 64, 1))
            j1 = jnp.where(low8, pltpu.roll(first, 64, 1), second)
            blocks[mx, my, b, ri] = jnp.concatenate([j0, j1], axis=0).astype(BF16)

    spread_copies = []
    for d, x, y, peer in plane:
        copy = pltpu.make_async_remote_copy(
            src_ref=blocks.at[mx, my], dst_ref=blocks.at[mx, my], send_sem=bs_sem.at[d],
            recv_sem=br_sem.at[d], device_id=peer, device_id_type=MESH,
        )
        copy.start()
        spread_copies.append(copy)
    for copy in back_copies:
        copy.wait_send()

    low16 = lax.broadcasted_iota(jnp.int32, (16, 128), 1) < 64
    pair_copies = []
    for dy in (0, 1, 3, 2):
        for dx in range(4):
            d = dy * 4 + dx
            if d:
                spread_copies[d - 1].wait_recv()
        y = (my + 4 - dy) % 4
        for b in range(2):
            for ri in range(2):
                for h in range(2):
                    even = blocks[2 * h, y, b, ri].astype(F32)
                    odd = blocks[2 * h + 1, y, b, ri].astype(F32)
                    near = jnp.where(low16, even, pltpu.roll(odd, 64, 1))
                    far = jnp.where(low16, pltpu.roll(even, 64, 1), odd)
                    spread[mc, y, b, ri, :, pl.ds(h * 128, 128)] = near.astype(BF16)
                    spread[mc, y, b, ri, :, pl.ds(256 + h * 128, 128)] = far.astype(BF16)
        copy = pltpu.make_async_remote_copy(
            src_ref=spread.at[mc, y], dst_ref=spread.at[mc, y], send_sem=as_sem.at[dy],
            recv_sem=ar_sem.at[dy], device_id=sibling, device_id_type=MESH,
        )
        copy.start()
        pair_copies.append(copy)
    for copy in spread_copies:
        copy.wait_send()
    for copy in pair_copies:
        copy.wait_recv()

    stores = []
    for b in range(2):
        modes = spread[:, :, b].reshape(256, WIDTH)
        for h in range(2):
            cells = pl.ds(h * 256, 256)
            spectral = jnp.dot(basis_t[cells, :], modes, preferred_element_type=F32)
            active = gelu(spectral * FIELD_SCALE + pre[b, cells, :]).astype(BF16)
            hidden = jnp.dot(active, inner_t[...], preferred_element_type=F32)
            hidden = gelu(hidden).astype(BF16)
            added = jnp.dot(hidden, outer[...], preferred_element_type=F32)
            result[b, cells, :] = (active.astype(F32) + added).astype(BF16)
            copy = pltpu.make_async_copy(
                result.at[b, cells], out_hbm.at[b, cells], store_sem.at[b * 2 + h]
            )
            copy.start()
            stores.append(copy)
    for copy in pair_copies:
        copy.wait_send()
    for copy in stores:
        copy.wait()


def local(grid_field, spectral_weight, skip_weight, inner_weight, outer_weight):
    table = jnp.asarray(local_tables())
    field = grid_field.reshape(2, CELLS, WIDTH)
    weight = jnp.swapaxes(spectral_weight, 2, 3)
    dma = pltpu.SemaphoreType.DMA
    out = pl.pallas_call(
        body,
        out_shape=jax.ShapeDtypeStruct((2, CELLS, WIDTH), BF16),
        in_specs=[pl.BlockSpec(memory_space=pltpu.HBM)] * 6,
        out_specs=pl.BlockSpec(memory_space=pltpu.HBM),
        scratch_shapes=[
            pltpu.VMEM((2, CELLS, WIDTH), BF16),
            pltpu.VMEM((2, 128, WIDTH), BF16),
            pltpu.VMEM((WIDTH, WIDTH), BF16),
            pltpu.VMEM((HIDDEN, WIDTH), BF16),
            pltpu.VMEM((HIDDEN, WIDTH), BF16),
            pltpu.VMEM((2, 4, 2, 16, CELLS), F32),
            pltpu.VMEM((2, 4, 2, 16, CELLS), BF16),
            pltpu.VMEM((CELLS, 256), BF16),
            pltpu.VMEM((WIDTH, HIDDEN), BF16),
            pltpu.VMEM((2, CELLS, WIDTH), F32),
            pltpu.VMEM((2, 128, WIDTH), BF16),
            pltpu.VMEM((2, 128, WIDTH), BF16),
            pltpu.VMEM((2, 128, WIDTH), F32),
            pltpu.VMEM((2, 4, 4, 32, 128), BF16),
            pltpu.VMEM((2, 16, 32, 128), BF16),
            pltpu.VMEM((64, 128), F32),
            pltpu.VMEM((16, 8, 128), F32),
            pltpu.VMEM((8, 128), F32),
            pltpu.VMEM((4, 8, 128), F32),
            pltpu.VMEM((8, 128), F32),
            pltpu.VMEM((128, 128), F32),
            pltpu.VMEM((4, 4, 2, 2, 16, 128), BF16),
            pltpu.VMEM((2, 4, 2, 2, 16, WIDTH), BF16),
            pltpu.VMEM((2, CELLS, WIDTH), BF16),
            dma((12,)),
            dma((2,)), dma((2,)),
            dma((2, 16)), dma((2, 16)),
            dma((16,)), dma((16,)),
            dma((4,)), dma((4,)),
            dma((16,)), dma((16,)),
            dma((16,)), dma((16,)),
            dma((4,)), dma((4,)),
            dma((4,)),
            pltpu.SemaphoreType.REGULAR, pltpu.SemaphoreType.REGULAR, pltpu.SemaphoreType.REGULAR,
        ],
        compiler_params=pltpu.CompilerParams(
            collective_id=0, has_side_effects=True, vmem_limit_bytes=63_000_000
        ),
        cost_estimate=pl.CostEstimate(flops=3_400_000_000, bytes_accessed=7 << 20, transcendentals=1_600_000),
    )(field, weight, skip_weight, inner_weight, outer_weight, table)
    return out.reshape(grid_field.shape)


def solution(mesh):
    in_specs = (P(None, "gx", "gy", None), P("gx", None, None, "gy"), P(), P(), P())
    out_specs = P(None, "gx", "gy", None)
    return jax.shard_map(local, mesh=mesh, in_specs=in_specs, out_specs=out_specs, check_vma=False)
```

```python
import math

import numpy as np
import jax
import jax.numpy as jnp
from jax import lax
from jax.experimental import pallas as pl
from jax.experimental.pallas import tpu as pltpu
from jax.sharding import PartitionSpec as P

MESH = pl.DeviceIdType.MESH
F32 = jnp.float32
BF16 = jnp.bfloat16
KX = 16
KY = 8
ROWS = 16
COLS = 32
CELLS = ROWS * COLS
NX = 1024
NY = 256
WIDTH = 512
HIDDEN = 1024
SPECTRUM_SCALE = 1.0 / math.sqrt(NX * NY)
FIELD_SCALE = 1.0 / math.sqrt(KX * KY)


def local_tables():
    core, y, j, z = np.meshgrid(np.arange(2), np.arange(4), np.arange(2), np.arange(8), indexing="ij")
    kx = (y * 4 + z // 2).reshape(2, 4, 16, 1, 1)
    ky = ((z % 2) * 4 + core * 2 + j).reshape(2, 4, 16, 1, 1)
    dx = np.arange(ROWS).reshape(1, 1, 1, ROWS, 1)
    dy = np.arange(COLS).reshape(1, 1, 1, 1, COLS)
    angle = 2.0 * np.pi * (kx * dx / NX + ky * dy / NY)
    angle = angle.reshape(2, 4, 16, CELLS)
    return np.stack([np.cos(angle), np.sin(angle)], axis=2).astype(np.float32)


def gelu(v):
    a = math.sqrt(2.0 / math.pi)
    t = jnp.tanh(v * (a + (a * 0.044715) * (v * v)))
    h = 0.5 * v
    return h + h * t


def body(
    field_hbm, weight_hbm, skip_hbm, inner_hbm, outer_hbm, table_hbm, out_ref,
    field, wv, skip, inner, outer, table,
    basis, basis_t, inner_t, pre,
    csend, crecv, own, xsend, xrecv, zsend, zrecv, gsend, grecv, held, spread,
    load_sem, cs_sem, cr_sem, xs_sem, xr_sem, zs_sem, zr_sem, ss_sem, sr_sem,
    gs_sem, gr_sem, bs_sem, br_sem, as_sem, ar_sem, across_ready, near_ready, far_ready,
):
    gx, gy = lax.axis_index("gx"), lax.axis_index("gy")
    my, mzl, mc = gx // 16, (gx // 2) % 8, gx % 2
    mzh, mx = gy // 4, gy % 4
    mz = mzh * 8 + mzl

    def at(y, z, c, x):
        return (y * 16 + (z % 8) * 2 + c, (z // 8) * 4 + x)

    sibling = at(my, mz, 1 - mc, mx)
    def partner(x, y):
        return at(y % 4, mz, mc, x % 4)

    steps = (10, 6, 14, 9, 11, 5, 7, 13, 15, 2, 8, 1, 3, 4, 12)
    batch, half = mx // 2, mx % 2
    column = []
    for d in (8, 7, 9, 6, 10, 5, 11, 4, 12, 3, 13, 2, 14, 1, 15):
        z = (mz + d) % 16
        column.append((d, z, at(my, z, mc, mx)))
    row = []
    for d in (2, 1, 3):
        x = (mx + d) % 4
        row.append((d, x, at(my, mz, mc, x)))

    def signal(semaphore, peers):
        for peer in peers:
            pl.semaphore_signal(semaphore, inc=1, device_id=peer, device_id_type=MESH)

    barrier = pltpu.get_barrier_semaphore()
    across = [at((my + d) % 4, mz, mc, mx) for d in (2, 1, 3)]
    along = {d: at(my, (mz + d) % 16, mc, mx) for d in (1, 2, 4, 12, 14, 15)}
    near = [sibling] + [p[-1] for p in row] + across + [along[d] for d in (2, 14, 1, 15)]
    signal(barrier, near)

    loads = []

    def load(src, dst):
        copy = pltpu.make_async_copy(src, dst, load_sem.at[len(loads)])
        copy.start()
        loads.append(copy)
        return copy

    first_in = load(table_hbm.at[1 - mc], table.at[1 - mc])
    field_in = [load(field_hbm.at[b], field.at[b]) for b in range(2)]
    second_in = load(table_hbm.at[mc], table.at[mc])

    index = lax.broadcasted_iota(jnp.int32, (16, 128), 0)
    lane = lax.broadcasted_iota(jnp.int32, (16, 128), 1)
    kx = (lane % 4) * 4 + (index % 8) // 2
    ky = (index % 2) * 4 + jnp.where(lane < 4, 1 - mc, mc) * 2 + index // 8
    x_phase = ((kx * (gx * ROWS)) % NX).astype(F32) * (1.0 / NX)
    y_phase = ((ky * (gy * COLS)) % NY).astype(F32) * (1.0 / NY)
    phase = x_phase + y_phase
    phase = jnp.where(phase >= 1.0, phase - 1.0, phase)
    phase = jnp.where(phase >= 0.5, phase - 1.0, phase)
    cos0 = jnp.cos(phase * (2.0 * math.pi))
    sin0 = jnp.sin(phase * (2.0 * math.pi))

    def make_basis(core, column0):
        for y in range(4):
            at_lane = slice(column0 + y, column0 + y + 1)
            c0 = jnp.broadcast_to(cos0[:, at_lane], (16, 128))
            s0 = jnp.broadcast_to(sin0[:, at_lane], (16, 128))
            for t in range(4):
                lanes = pl.ds(t * 128, 128)
                cd = table[core, y, 0, :, lanes]
                sd = table[core, y, 1, :, lanes]
                re = c0 * cd - s0 * sd
                im = -(s0 * cd + c0 * sd)
                for j in range(2):
                    rows = slice(j * 8, j * 8 + 8)
                    both = jnp.concatenate([re[rows], im[rows]], axis=0)
                    basis[core, y, j, :, lanes] = both.astype(BF16)

    def forward(core, b):
        rows = basis[core].reshape(128, CELLS)
        return jnp.dot(rows, field[b], preferred_element_type=F32)

    first_in.wait()
    make_basis(1 - mc, 0)
    core_copies = []
    for b in range(2):
        field_in[b].wait()
        part = forward(1 - mc, b)
        csend[b] = part.astype(BF16)
        if b == 0:
            pl.semaphore_wait(barrier, 11)
            signal(across_ready, across)
            signal(near_ready, [along[2], along[14]])
        copy = pltpu.make_async_remote_copy(
            src_ref=csend.at[b], dst_ref=crecv.at[b], send_sem=cs_sem.at[b], recv_sem=cr_sem.at[b],
            device_id=sibling, device_id_type=MESH,
        )
        copy.start()
        core_copies.append(copy)
    weight_in = load(weight_hbm.at[half], wv.at[:, pl.ds(pl.multiple_of(mx * 64, 64), 64)])
    skip_in = load(skip_hbm, skip)
    inner_in = load(inner_hbm, inner)
    outer_in = load(outer_hbm, outer)
    second_in.wait()
    make_basis(mc, 4)
    for b in range(2):
        own[b] = forward(mc, b)

    def plane_copy(x, dx, y, dy):
        return pltpu.make_async_remote_copy(
            src_ref=xsend.at[x // 2, (y % 4) * 2 + x % 2], dst_ref=xrecv.at[dy * 4 + dx],
            send_sem=xs_sem.at[dy * 4 + dx], recv_sem=xr_sem.at[dy * 4 + dx],
            device_id=partner(x, y), device_id_type=MESH,
        )

    for b in range(2):
        core_copies[b].wait_recv()
        xsend[b] = (own[b] + crecv[b].astype(F32)).astype(BF16).reshape(8, 16, WIDTH)
        if b == 0:
            pl.semaphore_wait(across_ready, 3)
        for dy in (2, 1, 3, 0):
            for x in (2 * b, 2 * b + 1):
                dx = (x + 4 - mx) % 4
                if dy:
                    plane_copy(x, dx, my + dy, dy).start()
                else:

                    @pl.when(dx != 0)
                    def _():
                        plane_copy(x, dx, my, 0).start()

    pl.semaphore_wait(near_ready, 2)
    signal(far_ready, [along[4], along[12]])
    skip_in.wait()
    for b in range(2):
        pre[b] = jnp.dot(field[b], skip[...], preferred_element_type=F32)

    row_copies = []
    for d, x, peer in row:
        copy = pltpu.make_async_remote_copy(
            src_ref=weight_hbm.at[x % 2], dst_ref=wv.at[:, pl.ds(pl.multiple_of(mx * 64, 64), 64)],
            send_sem=ss_sem.at[d], recv_sem=sr_sem.at[d], device_id=peer, device_id_type=MESH,
        )
        copy.start()
        row_copies.append(copy)

    mine = pl.ds(pl.multiple_of((my * 2 + half) * 16, 16), 16)
    total = own[batch, mine, :] + crecv[batch, mine, :].astype(F32)
    plane_copies = [plane_copy((mx + d) % 4, d % 4, my + d // 4, d // 4) for d in steps]
    for copy, d in reversed(list(zip(plane_copies, steps))):
        copy.wait_recv()
        total = total + xrecv[d].astype(F32)
    for ri in range(2):
        for t in range(4):
            zsend[pl.ds(ri * 4 + t, 8, stride=8), :] = total[ri * 8 : ri * 8 + 8, t * 128 : t * 128 + 128]

    pl.semaphore_wait(far_ready, 2)
    column_copies = []
    for d, z, peer in column:
        copy = pltpu.make_async_remote_copy(
            src_ref=zsend.at[pl.ds(pl.multiple_of((z % 8) * 8, 8), 8)], dst_ref=zrecv.at[d],
            send_sem=zs_sem.at[d], recv_sem=zr_sem.at[d], device_id=peer, device_id_type=MESH,
        )
        copy.start()
        column_copies.append(copy)

    for t in range(4):
        cells = pl.ds(t * 128, 128)
        basis_t[cells, :] = basis[:, :, :, :, cells].reshape(256, 128).T
    inner_in.wait()
    for t in range(8):
        units = pl.ds(t * 128, 128)
        inner_t[:, units] = inner[units, :].T
    for copy in core_copies + plane_copies:
        copy.wait_send()

    total = zsend[pl.ds(pl.multiple_of(mzl * 8, 8), 8), :]
    for copy, (d, _, _) in reversed(list(zip(column_copies, column))):
        copy.wait_recv()
        total = total + zrecv[d]
    spectrum = (total * SPECTRUM_SCALE).astype(BF16).astype(F32)

    weight_in.wait()
    for copy in row_copies:
        copy.wait_recv()
    parts = [
        jnp.concatenate([spectrum[ri * 4 + t : ri * 4 + t + 1] for t in range(4)], axis=1)
        for ri in range(2)
    ]
    modes = jnp.concatenate(parts * 4, axis=0).astype(BF16)
    nt = (((1,), (1,)), ((), ()))
    by_re = lax.dot_general(modes, wv[0], nt, preferred_element_type=F32)
    by_im = lax.dot_general(modes, wv[1], nt, preferred_element_type=F32)
    mixed_re = by_re[0:1] - by_im[1:2]
    mixed_im = by_im[0:1] + by_re[1:2]
    mixed = [v[:, t * 128 : t * 128 + 128] for v in (mixed_re, mixed_im) for t in range(2)]
    mixed = jnp.concatenate(mixed + mixed, axis=0).astype(BF16).astype(F32)

    gsend[...] = mixed
    back_copies = []
    for d, z, peer in column:
        copy = pltpu.make_async_remote_copy(
            src_ref=gsend, dst_ref=grecv.at[pl.ds(pl.multiple_of(mz * 8, 8), 8)],
            send_sem=gs_sem.at[d], recv_sem=gr_sem.at[d], device_id=peer, device_id_type=MESH,
        )
        copy.start()
        back_copies.append(copy)
    grecv[pl.ds(pl.multiple_of(mz * 8, 8), 8), :] = mixed
    outer_in.wait()
    for copy in column_copies + row_copies:
        copy.wait_send()
    for copy in reversed(back_copies):
        copy.wait_recv()

    for ri in range(2):
        for h in range(2):
            for t in range(2):
                part = grecv[pl.ds(h * 64 + ri * 2 + t, 8, stride=8), :]
                held[ri * 8 : ri * 8 + 8, pl.ds(h * 256 + t * 128, 128)] = part
    spread[mc, my, batch, half] = held[...].astype(BF16)

    spread_copies = {}
    block = spread.at[mc, my, batch, half]
    for d in steps:
        copy = pltpu.make_async_remote_copy(
            src_ref=block, dst_ref=block, send_sem=bs_sem.at[d], recv_sem=br_sem.at[d],
            device_id=partner(mx + d % 4, my + d // 4), device_id_type=MESH,
        )
        copy.start()
        spread_copies[d] = copy
    for copy in back_copies:
        copy.wait_send()

    pair_copies = []
    for dy in (0, 1, 3, 2):
        for dx in range(4):
            d = dy * 4 + dx
            if d:
                spread_copies[d].wait_recv()
        y = (my + 4 - dy) % 4
        copy = pltpu.make_async_remote_copy(
            src_ref=spread.at[mc, y], dst_ref=spread.at[mc, y], send_sem=as_sem.at[dy],
            recv_sem=ar_sem.at[dy], device_id=sibling, device_id_type=MESH,
        )
        copy.start()
        pair_copies.append(copy)
    for copy in spread_copies.values():
        copy.wait_send()
    for copy in pair_copies:
        copy.wait_recv()
    for copy in pair_copies:
        copy.wait_send()

    for b in range(2):
        modes = spread[:, :, b].reshape(256, WIDTH)
        for h in range(2):
            cells = pl.ds(h * 256, 256)
            spectral = jnp.dot(basis_t[cells, :], modes, preferred_element_type=F32)
            active = gelu(spectral * FIELD_SCALE + pre[b, cells, :]).astype(BF16)
            hidden = jnp.dot(active, inner_t[...], preferred_element_type=F32)
            hidden = gelu(hidden).astype(BF16)
            added = jnp.dot(hidden, outer[...], preferred_element_type=F32)
            out_ref[b, cells, :] = (active.astype(F32) + added).astype(BF16)


def local(grid_field, spectral_weight, skip_weight, inner_weight, outer_weight):
    table = jnp.asarray(local_tables())
    field = grid_field.reshape(2, CELLS, WIDTH)
    weight = jnp.swapaxes(spectral_weight, 2, 3)
    dma = pltpu.SemaphoreType.DMA
    operands = (field, weight, skip_weight, inner_weight, outer_weight, table)
    operands = [pltpu.with_memory_space_constraint(v, pltpu.HBM) for v in operands]
    out = pl.pallas_call(
        body,
        out_shape=jax.ShapeDtypeStruct((2, CELLS, WIDTH), BF16),
        in_specs=[pl.BlockSpec(memory_space=pltpu.HBM)] * 6,
        out_specs=pl.BlockSpec(memory_space=pltpu.VMEM),
        scratch_shapes=[
            pltpu.VMEM((2, CELLS, WIDTH), BF16),
            pltpu.VMEM((2, 256, WIDTH), BF16),
            pltpu.VMEM((WIDTH, WIDTH), BF16),
            pltpu.VMEM((HIDDEN, WIDTH), BF16),
            pltpu.VMEM((HIDDEN, WIDTH), BF16),
            pltpu.VMEM((2, 4, 2, 16, CELLS), F32),
            pltpu.VMEM((2, 4, 2, 16, CELLS), BF16),
            pltpu.VMEM((CELLS, 256), BF16),
            pltpu.VMEM((WIDTH, HIDDEN), BF16),
            pltpu.VMEM((2, CELLS, WIDTH), F32),
            pltpu.VMEM((2, 128, WIDTH), BF16),
            pltpu.VMEM((2, 128, WIDTH), BF16),
            pltpu.VMEM((2, 128, WIDTH), F32),
            pltpu.VMEM((2, 8, 16, WIDTH), BF16),
            pltpu.VMEM((16, 16, WIDTH), BF16),
            pltpu.VMEM((64, 128), F32),
            pltpu.VMEM((16, 8, 128), F32),
            pltpu.VMEM((8, 128), F32),
            pltpu.VMEM((128, 128), F32),
            pltpu.VMEM((16, WIDTH), F32),
            pltpu.VMEM((2, 4, 2, 2, 16, WIDTH), BF16),
            dma((12,)),
            dma((2,)), dma((2,)),
            dma((16,)), dma((16,)),
            dma((16,)), dma((16,)),
            dma((4,)), dma((4,)),
            dma((16,)), dma((16,)),
            dma((16,)), dma((16,)),
            dma((4,)), dma((4,)),
            pltpu.SemaphoreType.REGULAR, pltpu.SemaphoreType.REGULAR, pltpu.SemaphoreType.REGULAR,
        ],
        compiler_params=pltpu.CompilerParams(
            collective_id=0, has_side_effects=True, vmem_limit_bytes=40 << 20
        ),
        cost_estimate=pl.CostEstimate(flops=3_400_000_000, bytes_accessed=7 << 20, transcendentals=1_600_000),
    )(*operands)
    return out.reshape(grid_field.shape)


def solution(mesh):
    in_specs = (P(None, "gx", "gy", None), P("gx", None, None, "gy"), P(), P(), P())
    out_specs = P(None, "gx", "gy", None)
    return jax.shard_map(local, mesh=mesh, in_specs=in_specs, out_specs=out_specs, check_vma=False)
```

```python
import math

import numpy as np
import jax
import jax.numpy as jnp
from jax import lax
from jax.experimental import pallas as pl
from jax.experimental.pallas import tpu as pltpu
from jax.sharding import PartitionSpec as P

MESH = pl.DeviceIdType.MESH
F32 = jnp.float32
BF16 = jnp.bfloat16
KX = 16
KY = 8
ROWS = 16
COLS = 32
CELLS = ROWS * COLS
NX = 1024
NY = 256
WIDTH = 512
HIDDEN = 1024
SPECTRUM_SCALE = 1.0 / math.sqrt(NX * NY)
FIELD_SCALE = 1.0 / math.sqrt(KX * KY)


def local_tables():
    core, y, j, z = np.meshgrid(np.arange(2), np.arange(4), np.arange(2), np.arange(8), indexing="ij")
    kx = (y * 4 + z // 2).reshape(2, 4, 16, 1, 1)
    ky = ((z % 2) * 4 + core * 2 + j).reshape(2, 4, 16, 1, 1)
    dx = np.arange(ROWS).reshape(1, 1, 1, ROWS, 1)
    dy = np.arange(COLS).reshape(1, 1, 1, 1, COLS)
    angle = 2.0 * np.pi * (kx * dx / NX + ky * dy / NY)
    angle = angle.reshape(2, 4, 16, CELLS)
    return np.stack([np.cos(angle), np.sin(angle)], axis=2).astype(np.float32)


def gelu(v):
    a = math.sqrt(2.0 / math.pi)
    t = jnp.tanh(v * (a + (a * 0.044715) * (v * v)))
    h = 0.5 * v
    return h + h * t


def body(
    field_hbm, weight_hbm, skip_hbm, inner_hbm, outer_hbm, table_hbm, out_ref,
    field, wv, skip, inner, outer, table,
    basis, basis_t, inner_t, pre,
    csend, crecv, own, xsend, xrecv, zsend, zrecv, gsend, grecv, held, spread,
    load_sem, cs_sem, cr_sem, xs_sem, xr_sem, zs_sem, zr_sem, ss_sem, sr_sem,
    gs_sem, gr_sem, bs_sem, br_sem, as_sem, ar_sem, across_ready, near_ready, far_ready,
):
    gx, gy = lax.axis_index("gx"), lax.axis_index("gy")
    my, mzl, mc = gx // 16, (gx // 2) % 8, gx % 2
    mzh, mx = gy // 4, gy % 4
    mz = mzh * 8 + mzl

    def at(y, z, c, x):
        return (y * 16 + (z % 8) * 2 + c, (z // 8) * 4 + x)

    sibling = at(my, mz, 1 - mc, mx)
    def partner(x, y):
        return at(y % 4, mz, mc, x % 4)

    steps = (10, 6, 14, 9, 11, 5, 7, 13, 15, 2, 8, 1, 3, 4, 12)
    batch, half = mx // 2, mx % 2
    column = []
    for d in (8, 7, 9, 6, 10, 5, 11, 4, 12, 3, 13, 2, 14, 1, 15):
        z = (mz + d) % 16
        column.append((d, z, at(my, z, mc, mx)))
    row = []
    for d in (2, 1, 3):
        x = (mx + d) % 4
        row.append((d, x, at(my, mz, mc, x)))

    def signal(semaphore, peers):
        for peer in peers:
            pl.semaphore_signal(semaphore, inc=1, device_id=peer, device_id_type=MESH)

    barrier = pltpu.get_barrier_semaphore()
    across = [at((my + d) % 4, mz, mc, mx) for d in (2, 1, 3)]
    along = {d: at(my, (mz + d) % 16, mc, mx) for d in (1, 2, 4, 12, 14, 15)}
    near = [sibling] + [p[-1] for p in row] + across + [along[d] for d in (2, 14, 1, 15)]
    signal(barrier, near)

    loads = []

    def load(src, dst):
        copy = pltpu.make_async_copy(src, dst, load_sem.at[len(loads)])
        copy.start()
        loads.append(copy)
        return copy

    first_in = load(table_hbm.at[1 - mc], table.at[1 - mc])
    field_in = [load(field_hbm.at[b], field.at[b]) for b in range(2)]
    second_in = load(table_hbm.at[mc], table.at[mc])

    index = lax.broadcasted_iota(jnp.int32, (16, 128), 0)
    lane = lax.broadcasted_iota(jnp.int32, (16, 128), 1)
    kx = (lane % 4) * 4 + (index % 8) // 2
    ky = (index % 2) * 4 + jnp.where(lane < 4, 1 - mc, mc) * 2 + index // 8
    x_phase = ((kx * (gx * ROWS)) % NX).astype(F32) * (1.0 / NX)
    y_phase = ((ky * (gy * COLS)) % NY).astype(F32) * (1.0 / NY)
    phase = x_phase + y_phase
    phase = jnp.where(phase >= 1.0, phase - 1.0, phase)
    phase = jnp.where(phase >= 0.5, phase - 1.0, phase)
    cos0 = jnp.cos(phase * (2.0 * math.pi))
    sin0 = jnp.sin(phase * (2.0 * math.pi))

    def make_basis(core, column0):
        for y in range(4):
            at_lane = slice(column0 + y, column0 + y + 1)
            c0 = jnp.broadcast_to(cos0[:, at_lane], (16, 128))
            s0 = jnp.broadcast_to(sin0[:, at_lane], (16, 128))
            for t in range(4):
                lanes = pl.ds(t * 128, 128)
                cd = table[core, y, 0, :, lanes]
                sd = table[core, y, 1, :, lanes]
                re = c0 * cd - s0 * sd
                im = -(s0 * cd + c0 * sd)
                for j in range(2):
                    rows = slice(j * 8, j * 8 + 8)
                    both = jnp.concatenate([re[rows], im[rows]], axis=0)
                    basis[core, y, j, :, lanes] = both.astype(BF16)

    def forward(core, b):
        rows = basis[core].reshape(128, CELLS)
        return jnp.dot(rows, field[b], preferred_element_type=F32)

    first_in.wait()
    make_basis(1 - mc, 0)
    core_copies = []
    for b in range(2):
        field_in[b].wait()
        part = forward(1 - mc, b)
        csend[b] = part.astype(BF16)
        if b == 0:
            pl.semaphore_wait(barrier, 11)
            signal(across_ready, across)
            signal(near_ready, [along[2], along[14]])
        copy = pltpu.make_async_remote_copy(
            src_ref=csend.at[b], dst_ref=crecv.at[b], send_sem=cs_sem.at[b], recv_sem=cr_sem.at[b],
            device_id=sibling, device_id_type=MESH,
        )
        copy.start()
        core_copies.append(copy)
    weight_in = load(weight_hbm.at[half], wv.at[:, pl.ds(pl.multiple_of(mx * 64, 64), 64)])
    skip_in = load(skip_hbm, skip)
    inner_in = load(inner_hbm, inner)
    outer_in = load(outer_hbm, outer)
    second_in.wait()
    make_basis(mc, 4)
    own[0] = forward(mc, 0)

    def plane_copy(x, dx, y, dy):
        return pltpu.make_async_remote_copy(
            src_ref=xsend.at[x // 2, (y % 4) * 2 + x % 2], dst_ref=xrecv.at[dy * 4 + dx],
            send_sem=xs_sem.at[dy * 4 + dx], recv_sem=xr_sem.at[dy * 4 + dx],
            device_id=partner(x, y), device_id_type=MESH,
        )

    for b in range(2):
        if b == 1:
            own[1] = forward(mc, 1)
        core_copies[b].wait_recv()
        xsend[b] = (own[b] + crecv[b].astype(F32)).astype(BF16).reshape(8, 16, WIDTH)
        if b == 0:
            pl.semaphore_wait(across_ready, 3)
        for dy in (2, 1, 3, 0):
            for x in (2 * b, 2 * b + 1):
                dx = (x + 4 - mx) % 4
                if dy:
                    plane_copy(x, dx, my + dy, dy).start()
                else:

                    @pl.when(dx != 0)
                    def _():
                        plane_copy(x, dx, my, 0).start()

    pl.semaphore_wait(near_ready, 2)
    signal(far_ready, [along[4], along[12]])
    skip_in.wait()
    for b in range(2):
        pre[b] = jnp.dot(field[b], skip[...], preferred_element_type=F32)

    row_copies = []
    for d, x, peer in row:
        copy = pltpu.make_async_remote_copy(
            src_ref=weight_hbm.at[x % 2], dst_ref=wv.at[:, pl.ds(pl.multiple_of(mx * 64, 64), 64)],
            send_sem=ss_sem.at[d], recv_sem=sr_sem.at[d], device_id=peer, device_id_type=MESH,
        )
        row_copies.append(copy)

    mine = pl.ds(pl.multiple_of((my * 2 + half) * 16, 16), 16)
    total = own[batch, mine, :] + crecv[batch, mine, :].astype(F32)
    plane_copies = [plane_copy((mx + d) % 4, d % 4, my + d // 4, d // 4) for d in steps]
    for copy, d in reversed(list(zip(plane_copies, steps))):
        copy.wait_recv()
        total = total + xrecv[d].astype(F32)
        if d == 7:
            for weights in row_copies:
                weights.start()
    for ri in range(2):
        for t in range(4):
            zsend[pl.ds(ri * 4 + t, 8, stride=8), :] = total[ri * 8 : ri * 8 + 8, t * 128 : t * 128 + 128]

    pl.semaphore_wait(far_ready, 2)
    column_copies = []
    for d, z, peer in column:
        copy = pltpu.make_async_remote_copy(
            src_ref=zsend.at[pl.ds(pl.multiple_of((z % 8) * 8, 8), 8)], dst_ref=zrecv.at[d],
            send_sem=zs_sem.at[d], recv_sem=zr_sem.at[d], device_id=peer, device_id_type=MESH,
        )
        copy.start()
        column_copies.append(copy)

    for t in range(4):
        cells = pl.ds(t * 128, 128)
        basis_t[cells, :] = basis[:, :, :, :, cells].reshape(256, 128).T
    inner_in.wait()
    for t in range(8):
        units = pl.ds(t * 128, 128)
        inner_t[:, units] = inner[units, :].T
    for copy in core_copies + plane_copies:
        copy.wait_send()

    total = zsend[pl.ds(pl.multiple_of(mzl * 8, 8), 8), :]
    for copy, (d, _, _) in reversed(list(zip(column_copies, column))):
        copy.wait_recv()
        total = total + zrecv[d]
    spectrum = (total * SPECTRUM_SCALE).astype(BF16).astype(F32)

    weight_in.wait()
    for copy in row_copies:
        copy.wait_recv()
    parts = [
        jnp.concatenate([spectrum[ri * 4 + t : ri * 4 + t + 1] for t in range(4)], axis=1)
        for ri in range(2)
    ]
    modes = jnp.concatenate(parts * 4, axis=0).astype(BF16)
    nt = (((1,), (1,)), ((), ()))
    by_re = lax.dot_general(modes, wv[0], nt, preferred_element_type=F32)
    by_im = lax.dot_general(modes, wv[1], nt, preferred_element_type=F32)
    mixed_re = by_re[0:1] - by_im[1:2]
    mixed_im = by_im[0:1] + by_re[1:2]
    mixed = [v[:, t * 128 : t * 128 + 128] for v in (mixed_re, mixed_im) for t in range(2)]
    mixed = jnp.concatenate(mixed + mixed, axis=0).astype(BF16).astype(F32)

    gsend[...] = mixed
    back_copies = []
    for d, z, peer in column:
        copy = pltpu.make_async_remote_copy(
            src_ref=gsend, dst_ref=grecv.at[pl.ds(pl.multiple_of(mz * 8, 8), 8)],
            send_sem=gs_sem.at[d], recv_sem=gr_sem.at[d], device_id=peer, device_id_type=MESH,
        )
        copy.start()
        back_copies.append(copy)
    grecv[pl.ds(pl.multiple_of(mz * 8, 8), 8), :] = mixed
    outer_in.wait()
    for copy in column_copies + row_copies:
        copy.wait_send()
    for copy in reversed(back_copies):
        copy.wait_recv()

    for ri in range(2):
        for h in range(2):
            for t in range(2):
                part = grecv[pl.ds(h * 64 + ri * 2 + t, 8, stride=8), :]
                held[ri * 8 : ri * 8 + 8, pl.ds(h * 256 + t * 128, 128)] = part
    spread[mc, my, batch, half] = held[...].astype(BF16)

    block = spread.at[mc, my, batch, half]

    def arrival(d):
        return pltpu.make_async_remote_copy(
            src_ref=block, dst_ref=block, send_sem=bs_sem.at[d], recv_sem=br_sem.at[d],
            device_id=partner(mx + d % 4, my + d // 4), device_id_type=MESH,
        )

    for d in steps:
        arrival(d).start()
    for copy in back_copies:
        copy.wait_send()

    pair_copies = [[], []]

    def pass_on(dy, b):
        y = (my + 4 - dy) % 4
        for x in (2 * b, 2 * b + 1):
            d = dy * 4 + (mx + 4 - x) % 4
            if dy:
                arrival(d).wait_recv()
            else:

                @pl.when(x != mx)
                def _():
                    arrival(d).wait_recv()

        copy = pltpu.make_async_remote_copy(
            src_ref=spread.at[mc, y, b], dst_ref=spread.at[mc, y, b],
            send_sem=as_sem.at[dy, b], recv_sem=ar_sem.at[dy, b],
            device_id=sibling, device_id_type=MESH,
        )
        copy.start()
        pair_copies[b].append(copy)

    def finish(b, h):
        modes = spread[:, :, b].reshape(256, WIDTH)
        cells = pl.ds(h * 256, 256)
        spectral = jnp.dot(basis_t[cells, :], modes, preferred_element_type=F32)
        active = gelu(spectral * FIELD_SCALE + pre[b, cells, :]).astype(BF16)
        hidden = jnp.dot(active, inner_t[...], preferred_element_type=F32)
        hidden = gelu(hidden).astype(BF16)
        added = jnp.dot(hidden, outer[...], preferred_element_type=F32)
        out_ref[b, cells, :] = (active.astype(F32) + added).astype(BF16)

    for dy in (0, 1, 3):
        pass_on(dy, 0)
        pass_on(dy, 1)
    pass_on(2, 0)
    for copy in pair_copies[0]:
        copy.wait_recv()
    finish(0, 0)
    pass_on(2, 1)
    finish(0, 1)
    for d in steps:
        arrival(d).wait_send()
    for copy in pair_copies[0] + pair_copies[1]:
        copy.wait_send()
    for copy in pair_copies[1]:
        copy.wait_recv()
    finish(1, 0)
    finish(1, 1)


def local(grid_field, spectral_weight, skip_weight, inner_weight, outer_weight):
    table = jnp.asarray(local_tables())
    field = grid_field.reshape(2, CELLS, WIDTH)
    weight = jnp.swapaxes(spectral_weight, 2, 3)
    dma = pltpu.SemaphoreType.DMA
    operands = (field, weight, skip_weight, inner_weight, outer_weight, table)
    operands = [pltpu.with_memory_space_constraint(v, pltpu.HBM) for v in operands]
    out = pl.pallas_call(
        body,
        out_shape=jax.ShapeDtypeStruct((2, CELLS, WIDTH), BF16),
        in_specs=[pl.BlockSpec(memory_space=pltpu.HBM)] * 6,
        out_specs=pl.BlockSpec(memory_space=pltpu.VMEM),
        scratch_shapes=[
            pltpu.VMEM((2, CELLS, WIDTH), BF16),
            pltpu.VMEM((2, 256, WIDTH), BF16),
            pltpu.VMEM((WIDTH, WIDTH), BF16),
            pltpu.VMEM((HIDDEN, WIDTH), BF16),
            pltpu.VMEM((HIDDEN, WIDTH), BF16),
            pltpu.VMEM((2, 4, 2, 16, CELLS), F32),
            pltpu.VMEM((2, 4, 2, 16, CELLS), BF16),
            pltpu.VMEM((CELLS, 256), BF16),
            pltpu.VMEM((WIDTH, HIDDEN), BF16),
            pltpu.VMEM((2, CELLS, WIDTH), F32),
            pltpu.VMEM((2, 128, WIDTH), BF16),
            pltpu.VMEM((2, 128, WIDTH), BF16),
            pltpu.VMEM((2, 128, WIDTH), F32),
            pltpu.VMEM((2, 8, 16, WIDTH), BF16),
            pltpu.VMEM((16, 16, WIDTH), BF16),
            pltpu.VMEM((64, 128), F32),
            pltpu.VMEM((16, 8, 128), F32),
            pltpu.VMEM((8, 128), F32),
            pltpu.VMEM((128, 128), F32),
            pltpu.VMEM((16, WIDTH), F32),
            pltpu.VMEM((2, 4, 2, 2, 16, WIDTH), BF16),
            dma((12,)),
            dma((2,)), dma((2,)),
            dma((16,)), dma((16,)),
            dma((16,)), dma((16,)),
            dma((4,)), dma((4,)),
            dma((16,)), dma((16,)),
            dma((16,)), dma((16,)),
            dma((4, 2)), dma((4, 2)),
            pltpu.SemaphoreType.REGULAR, pltpu.SemaphoreType.REGULAR, pltpu.SemaphoreType.REGULAR,
        ],
        compiler_params=pltpu.CompilerParams(
            collective_id=0, has_side_effects=True, vmem_limit_bytes=40 << 20
        ),
        cost_estimate=pl.CostEstimate(flops=3_400_000_000, bytes_accessed=7 << 20, transcendentals=1_600_000),
    )(*operands)
    return out.reshape(grid_field.shape)


def solution(mesh):
    in_specs = (P(None, "gx", "gy", None), P("gx", None, None, "gy"), P(), P(), P())
    out_specs = P(None, "gx", "gy", None)
    return jax.shard_map(local, mesh=mesh, in_specs=in_specs, out_specs=out_specs, check_vma=False)
```

```python
import math

import numpy as np
import jax
import jax.numpy as jnp
from jax import lax
from jax.experimental import pallas as pl
from jax.experimental.pallas import tpu as pltpu
from jax.sharding import PartitionSpec as P

MESH = pl.DeviceIdType.MESH
F32 = jnp.float32
BF16 = jnp.bfloat16
KX = 16
KY = 8
ROWS = 16
COLS = 32
CELLS = ROWS * COLS
NX = 1024
NY = 256
WIDTH = 512
HIDDEN = 1024
SPECTRUM_SCALE = 1.0 / math.sqrt(NX * NY)
FIELD_SCALE = 1.0 / math.sqrt(KX * KY)


def local_tables():
    core, y, j, z = np.meshgrid(np.arange(2), np.arange(4), np.arange(2), np.arange(8), indexing="ij")
    kx = (y * 4 + z // 2).reshape(2, 4, 16, 1, 1)
    ky = ((z % 2) * 4 + core * 2 + j).reshape(2, 4, 16, 1, 1)
    dx = np.arange(ROWS).reshape(1, 1, 1, ROWS, 1)
    dy = np.arange(COLS).reshape(1, 1, 1, 1, COLS)
    angle = 2.0 * np.pi * (kx * dx / NX + ky * dy / NY)
    angle = angle.reshape(2, 4, 16, CELLS)
    return np.stack([np.cos(angle), np.sin(angle)], axis=2).astype(np.float32)


def gelu(v):
    a = math.sqrt(2.0 / math.pi)
    t = jnp.tanh(v * (a + (a * 0.044715) * (v * v)))
    h = 0.5 * v
    return h + h * t


def body(
    field_hbm, weight_hbm, skip_hbm, inner_hbm, outer_hbm, table_hbm, out_ref, active_ref, hidden_ref, outer,
    field, wv, skip, inner, table,
    basis, basis_t, inner_t, pre,
    csend, crecv, own, xsend, xrecv, zsend, zrecv, gsend, grecv, held, spread,
    load_sem, cs_sem, cr_sem, xs_sem, xr_sem, zs_sem, zr_sem, ss_sem, sr_sem,
    gs_sem, gr_sem, bs_sem, br_sem, as_sem, ar_sem, across_ready, near_ready, far_ready,
):
    gx, gy = lax.axis_index("gx"), lax.axis_index("gy")
    my, mzl, mc = gx // 16, (gx // 2) % 8, gx % 2
    mzh, mx = gy // 4, gy % 4
    mz = mzh * 8 + mzl

    def at(y, z, c, x):
        return (y * 16 + (z % 8) * 2 + c, (z // 8) * 4 + x)

    sibling = at(my, mz, 1 - mc, mx)
    def partner(x, y):
        return at(y % 4, mz, mc, x % 4)

    steps = (10, 6, 14, 9, 11, 5, 7, 13, 15, 2, 8, 1, 3, 4, 12)
    batch, half = mx // 2, mx % 2
    column = []
    for d in (8, 7, 9, 6, 10, 5, 11, 4, 12, 3, 13, 2, 14, 1, 15):
        z = (mz + d) % 16
        column.append((d, z, at(my, z, mc, mx)))
    row = []
    for d in (2, 1, 3):
        x = (mx + d) % 4
        row.append((d, x, at(my, mz, mc, x)))

    def signal(semaphore, peers):
        for peer in peers:
            pl.semaphore_signal(semaphore, inc=1, device_id=peer, device_id_type=MESH)

    barrier = pltpu.get_barrier_semaphore()
    across = [at((my + d) % 4, mz, mc, mx) for d in (2, 1, 3)]
    along = {d: at(my, (mz + d) % 16, mc, mx) for d in (1, 2, 4, 12, 14, 15)}
    near = [sibling] + [p[-1] for p in row] + across + [along[d] for d in (2, 14, 1, 15)]
    signal(barrier, near)

    loads = []

    def load(src, dst):
        copy = pltpu.make_async_copy(src, dst, load_sem.at[len(loads)])
        copy.start()
        loads.append(copy)
        return copy

    first_in = load(table_hbm.at[1 - mc], table.at[1 - mc])
    field_in = [load(field_hbm.at[b], field.at[b]) for b in range(2)]
    second_in = load(table_hbm.at[mc], table.at[mc])

    index = lax.broadcasted_iota(jnp.int32, (16, 128), 0)
    lane = lax.broadcasted_iota(jnp.int32, (16, 128), 1)
    kx = (lane % 4) * 4 + (index % 8) // 2
    ky = (index % 2) * 4 + jnp.where(lane < 4, 1 - mc, mc) * 2 + index // 8
    x_phase = ((kx * (gx * ROWS)) % NX).astype(F32) * (1.0 / NX)
    y_phase = ((ky * (gy * COLS)) % NY).astype(F32) * (1.0 / NY)
    phase = x_phase + y_phase
    phase = jnp.where(phase >= 1.0, phase - 1.0, phase)
    phase = jnp.where(phase >= 0.5, phase - 1.0, phase)
    cos0 = jnp.cos(phase * (2.0 * math.pi))
    sin0 = jnp.sin(phase * (2.0 * math.pi))

    def make_basis(core, column0):
        for y in range(4):
            at_lane = slice(column0 + y, column0 + y + 1)
            c0 = jnp.broadcast_to(cos0[:, at_lane], (16, 128))
            s0 = jnp.broadcast_to(sin0[:, at_lane], (16, 128))
            for t in range(4):
                lanes = pl.ds(t * 128, 128)
                cd = table[core, y, 0, :, lanes]
                sd = table[core, y, 1, :, lanes]
                re = c0 * cd - s0 * sd
                im = -(s0 * cd + c0 * sd)
                for j in range(2):
                    rows = slice(j * 8, j * 8 + 8)
                    both = jnp.concatenate([re[rows], im[rows]], axis=0)
                    basis[core, y, j, :, lanes] = both.astype(BF16)

    def forward(core, b):
        rows = basis[core].reshape(128, CELLS)
        return jnp.dot(rows, field[b], preferred_element_type=F32)

    first_in.wait()
    make_basis(1 - mc, 0)
    core_copies = []
    for b in range(2):
        field_in[b].wait()
        part = forward(1 - mc, b)
        csend[b] = part.astype(BF16)
        if b == 0:
            pl.semaphore_wait(barrier, 11)
            signal(across_ready, across)
            signal(near_ready, [along[2], along[14]])
        copy = pltpu.make_async_remote_copy(
            src_ref=csend.at[b], dst_ref=crecv.at[b], send_sem=cs_sem.at[b], recv_sem=cr_sem.at[b],
            device_id=sibling, device_id_type=MESH,
        )
        copy.start()
        core_copies.append(copy)
    weight_in = load(weight_hbm.at[half], wv.at[:, pl.ds(pl.multiple_of(mx * 64, 64), 64)])
    skip_in = load(skip_hbm, skip)
    inner_in = load(inner_hbm, inner)
    outer_in = load(outer_hbm, outer)
    second_in.wait()
    make_basis(mc, 4)
    own[0] = forward(mc, 0)

    def plane_copy(x, dx, y, dy):
        return pltpu.make_async_remote_copy(
            src_ref=xsend.at[x // 2, (y % 4) * 2 + x % 2], dst_ref=xrecv.at[dy * 4 + dx],
            send_sem=xs_sem.at[dy * 4 + dx], recv_sem=xr_sem.at[dy * 4 + dx],
            device_id=partner(x, y), device_id_type=MESH,
        )

    for b in range(2):
        if b == 1:
            own[1] = forward(mc, 1)
        core_copies[b].wait_recv()
        xsend[b] = (own[b] + crecv[b].astype(F32)).astype(BF16).reshape(8, 16, WIDTH)
        if b == 0:
            pl.semaphore_wait(across_ready, 3)
        for dy in (2, 1, 3, 0):
            for x in (2 * b, 2 * b + 1):
                dx = (x + 4 - mx) % 4
                if dy:
                    plane_copy(x, dx, my + dy, dy).start()
                else:

                    @pl.when(dx != 0)
                    def _():
                        plane_copy(x, dx, my, 0).start()

    pl.semaphore_wait(near_ready, 2)
    signal(far_ready, [along[4], along[12]])
    skip_in.wait()
    for b in range(2):
        pre[b] = jnp.dot(field[b], skip[...], preferred_element_type=F32)

    row_copies = []
    for d, x, peer in row:
        copy = pltpu.make_async_remote_copy(
            src_ref=weight_hbm.at[x % 2], dst_ref=wv.at[:, pl.ds(pl.multiple_of(mx * 64, 64), 64)],
            send_sem=ss_sem.at[d], recv_sem=sr_sem.at[d], device_id=peer, device_id_type=MESH,
        )
        row_copies.append(copy)

    mine = pl.ds(pl.multiple_of((my * 2 + half) * 16, 16), 16)
    total = own[batch, mine, :] + crecv[batch, mine, :].astype(F32)
    plane_copies = [plane_copy((mx + d) % 4, d % 4, my + d // 4, d // 4) for d in steps]
    for copy, d in reversed(list(zip(plane_copies, steps))):
        copy.wait_recv()
        total = total + xrecv[d].astype(F32)
        if d == 7:
            row_copies[0].start()
    for ri in range(2):
        for t in range(4):
            zsend[pl.ds(ri * 4 + t, 8, stride=8), :] = total[ri * 8 : ri * 8 + 8, t * 128 : t * 128 + 128]

    pl.semaphore_wait(far_ready, 2)
    column_copies = []
    for d, z, peer in column:
        copy = pltpu.make_async_remote_copy(
            src_ref=zsend.at[pl.ds(pl.multiple_of((z % 8) * 8, 8), 8)], dst_ref=zrecv.at[d],
            send_sem=zs_sem.at[d], recv_sem=zr_sem.at[d], device_id=peer, device_id_type=MESH,
        )
        copy.start()
        column_copies.append(copy)
    row_copies[1].start()
    row_copies[2].start()

    for t in range(4):
        cells = pl.ds(t * 128, 128)
        basis_t[cells, :] = basis[:, :, :, :, cells].reshape(256, 128).T
    inner_in.wait()
    for t in range(8):
        units = pl.ds(t * 128, 128)
        inner_t[:, units] = inner[units, :].T
    for copy in core_copies + plane_copies:
        copy.wait_send()

    total = zsend[pl.ds(pl.multiple_of(mzl * 8, 8), 8), :]
    for copy, (d, _, _) in reversed(list(zip(column_copies, column))):
        copy.wait_recv()
        total = total + zrecv[d]
    spectrum = (total * SPECTRUM_SCALE).astype(BF16).astype(F32)

    weight_in.wait()
    for copy in row_copies:
        copy.wait_recv()
    parts = [
        jnp.concatenate([spectrum[ri * 4 + t : ri * 4 + t + 1] for t in range(4)], axis=1)
        for ri in range(2)
    ]
    modes = jnp.concatenate(parts * 4, axis=0).astype(BF16)
    nt = (((1,), (1,)), ((), ()))
    by_re = lax.dot_general(modes, wv[0], nt, preferred_element_type=F32)
    by_im = lax.dot_general(modes, wv[1], nt, preferred_element_type=F32)
    mixed_re = by_re[0:1] - by_im[1:2]
    mixed_im = by_im[0:1] + by_re[1:2]
    mixed = [v[:, t * 128 : t * 128 + 128] for v in (mixed_re, mixed_im) for t in range(2)]
    mixed = jnp.concatenate(mixed + mixed, axis=0).astype(BF16).astype(F32)

    gsend[...] = mixed
    back_copies = []
    for d, z, peer in column:
        copy = pltpu.make_async_remote_copy(
            src_ref=gsend, dst_ref=grecv.at[pl.ds(pl.multiple_of(mz * 8, 8), 8)],
            send_sem=gs_sem.at[d], recv_sem=gr_sem.at[d], device_id=peer, device_id_type=MESH,
        )
        copy.start()
        back_copies.append(copy)
    grecv[pl.ds(pl.multiple_of(mz * 8, 8), 8), :] = mixed
    outer_in.wait()
    for copy in column_copies + row_copies:
        copy.wait_send()
    for copy in reversed(back_copies):
        copy.wait_recv()

    for ri in range(2):
        for h in range(2):
            for t in range(2):
                part = grecv[pl.ds(h * 64 + ri * 2 + t, 8, stride=8), :]
                held[ri * 8 : ri * 8 + 8, pl.ds(h * 256 + t * 128, 128)] = part
    spread[mc, my, batch, half] = held[...].astype(BF16)

    block = spread.at[mc, my, batch, half]

    def arrival(d):
        return pltpu.make_async_remote_copy(
            src_ref=block, dst_ref=block, send_sem=bs_sem.at[d], recv_sem=br_sem.at[d],
            device_id=partner(mx + d % 4, my + d // 4), device_id_type=MESH,
        )

    for d in steps:
        arrival(d).start()
    for copy in back_copies:
        copy.wait_send()

    pair_copies = [[], []]

    def pass_on(dy, b):
        y = (my + 4 - dy) % 4
        for x in (2 * b, 2 * b + 1):
            d = dy * 4 + (mx + 4 - x) % 4
            if dy:
                arrival(d).wait_recv()
            else:

                @pl.when(x != mx)
                def _():
                    arrival(d).wait_recv()

        copy = pltpu.make_async_remote_copy(
            src_ref=spread.at[mc, y, b], dst_ref=spread.at[mc, y, b],
            send_sem=as_sem.at[dy, b], recv_sem=ar_sem.at[dy, b],
            device_id=sibling, device_id_type=MESH,
        )
        copy.start()
        pair_copies[b].append(copy)

    def finish(b, h):
        modes = spread[:, :, b].reshape(256, WIDTH)
        cells = pl.ds(h * 256, 256)
        spectral = jnp.dot(basis_t[cells, :], modes, preferred_element_type=F32)
        active = gelu(spectral * FIELD_SCALE + pre[b, cells, :]).astype(BF16)
        hidden = jnp.dot(active, inner_t[...], preferred_element_type=F32)
        hidden = gelu(hidden).astype(BF16)
        if b == 0:
            added = jnp.dot(hidden, outer[...], preferred_element_type=F32)
            out_ref[cells, :] = (active.astype(F32) + added).astype(BF16)
        else:
            active_ref[cells, :] = active
            hidden_ref[cells, :] = hidden

    for dy in (0, 1, 3):
        pass_on(dy, 0)
        pass_on(dy, 1)
    pass_on(2, 0)
    for copy in pair_copies[0]:
        copy.wait_recv()
    finish(0, 0)
    pass_on(2, 1)
    finish(0, 1)
    for d in steps:
        arrival(d).wait_send()
    for copy in pair_copies[0] + pair_copies[1]:
        copy.wait_send()
    for copy in pair_copies[1]:
        copy.wait_recv()
    finish(1, 0)
    finish(1, 1)


def store(first, active, hidden, outer, out_hbm, second, sems):
    copies = [pltpu.make_async_copy(first, out_hbm.at[0], sems.at[0])]
    copies[0].start()
    for h in range(4):
        cells = pl.ds(h * 128, 128)
        added = jnp.dot(hidden[cells, :], outer[...], preferred_element_type=F32)
        second[cells, :] = (active[cells, :].astype(F32) + added).astype(BF16)
        copy = pltpu.make_async_copy(second.at[cells], out_hbm.at[1, cells], sems.at[1 + h])
        copy.start()
        copies.append(copy)
    for copy in copies:
        copy.wait()


def local(grid_field, spectral_weight, skip_weight, inner_weight, outer_weight):
    table = jnp.asarray(local_tables())
    field = grid_field.reshape(2, CELLS, WIDTH)
    weight = jnp.swapaxes(spectral_weight, 2, 3)
    dma = pltpu.SemaphoreType.DMA
    operands = (field, weight, skip_weight, inner_weight, outer_weight, table)
    operands = [pltpu.with_memory_space_constraint(v, pltpu.HBM) for v in operands]
    parts = pl.pallas_call(
        body,
        out_shape=[
            jax.ShapeDtypeStruct((CELLS, WIDTH), BF16),
            jax.ShapeDtypeStruct((CELLS, WIDTH), BF16),
            jax.ShapeDtypeStruct((CELLS, HIDDEN), BF16),
            jax.ShapeDtypeStruct((HIDDEN, WIDTH), BF16),
        ],
        in_specs=[pl.BlockSpec(memory_space=pltpu.HBM)] * 6,
        out_specs=[pl.BlockSpec(memory_space=pltpu.VMEM)] * 4,
        scratch_shapes=[
            pltpu.VMEM((2, CELLS, WIDTH), BF16),
            pltpu.VMEM((2, 256, WIDTH), BF16),
            pltpu.VMEM((WIDTH, WIDTH), BF16),
            pltpu.VMEM((HIDDEN, WIDTH), BF16),
            pltpu.VMEM((2, 4, 2, 16, CELLS), F32),
            pltpu.VMEM((2, 4, 2, 16, CELLS), BF16),
            pltpu.VMEM((CELLS, 256), BF16),
            pltpu.VMEM((WIDTH, HIDDEN), BF16),
            pltpu.VMEM((2, CELLS, WIDTH), F32),
            pltpu.VMEM((2, 128, WIDTH), BF16),
            pltpu.VMEM((2, 128, WIDTH), BF16),
            pltpu.VMEM((2, 128, WIDTH), F32),
            pltpu.VMEM((2, 8, 16, WIDTH), BF16),
            pltpu.VMEM((16, 16, WIDTH), BF16),
            pltpu.VMEM((64, 128), F32),
            pltpu.VMEM((16, 8, 128), F32),
            pltpu.VMEM((8, 128), F32),
            pltpu.VMEM((128, 128), F32),
            pltpu.VMEM((16, WIDTH), F32),
            pltpu.VMEM((2, 4, 2, 2, 16, WIDTH), BF16),
            dma((12,)),
            dma((2,)), dma((2,)),
            dma((16,)), dma((16,)),
            dma((16,)), dma((16,)),
            dma((4,)), dma((4,)),
            dma((16,)), dma((16,)),
            dma((16,)), dma((16,)),
            dma((4, 2)), dma((4, 2)),
            pltpu.SemaphoreType.REGULAR, pltpu.SemaphoreType.REGULAR, pltpu.SemaphoreType.REGULAR,
        ],
        compiler_params=pltpu.CompilerParams(
            collective_id=0, has_side_effects=True, vmem_limit_bytes=40 << 20
        ),
        cost_estimate=pl.CostEstimate(flops=3_400_000_000, bytes_accessed=7 << 20, transcendentals=1_600_000),
    )(*operands)
    out = pl.pallas_call(
        store,
        out_shape=jax.ShapeDtypeStruct((2, CELLS, WIDTH), BF16),
        in_specs=[pl.BlockSpec(memory_space=pltpu.VMEM)] * 4,
        out_specs=pl.BlockSpec(memory_space=pltpu.HBM),
        scratch_shapes=[pltpu.VMEM((CELLS, WIDTH), BF16), dma((5,))],
        compiler_params=pltpu.CompilerParams(vmem_limit_bytes=16 << 20),
    )(*parts)
    return out.reshape(grid_field.shape)


def solution(mesh):
    in_specs = (P(None, "gx", "gy", None), P("gx", None, None, "gy"), P(), P(), P())
    out_specs = P(None, "gx", "gy", None)
    return jax.shard_map(local, mesh=mesh, in_specs=in_specs, out_specs=out_specs, check_vma=False)
```

```python
import math

import numpy as np
import jax
import jax.numpy as jnp
from jax import lax
from jax.experimental import pallas as pl
from jax.experimental.pallas import tpu as pltpu
from jax.sharding import PartitionSpec as P

MESH = pl.DeviceIdType.MESH
F32 = jnp.float32
BF16 = jnp.bfloat16
KX = 16
KY = 8
ROWS = 16
COLS = 32
CELLS = ROWS * COLS
NX = 1024
NY = 256
WIDTH = 512
HIDDEN = 1024
SPECTRUM_SCALE = 1.0 / math.sqrt(NX * NY)
FIELD_SCALE = 1.0 / math.sqrt(KX * KY)


def local_tables():
    core, y, j, z = np.meshgrid(np.arange(2), np.arange(4), np.arange(2), np.arange(8), indexing="ij")
    kx = (y * 4 + z // 2).reshape(2, 4, 16, 1, 1)
    ky = ((z % 2) * 4 + core * 2 + j).reshape(2, 4, 16, 1, 1)
    dx = np.arange(ROWS).reshape(1, 1, 1, ROWS, 1)
    dy = np.arange(COLS).reshape(1, 1, 1, 1, COLS)
    angle = 2.0 * np.pi * (kx * dx / NX + ky * dy / NY)
    angle = angle.reshape(2, 4, 16, CELLS)
    return np.stack([np.cos(angle), np.sin(angle)], axis=2).astype(np.float32)


def gelu(v):
    a = math.sqrt(2.0 / math.pi)
    t = jnp.tanh(v * (a + (a * 0.044715) * (v * v)))
    h = 0.5 * v
    return h + h * t


def body(
    field_hbm, weight_hbm, skip_hbm, inner_hbm, outer_hbm, table_hbm, out_ref,
    field, wv, skip, inner, outer, table,
    basis, basis_t, inner_t, pre,
    csend, crecv, own, xsend, xrecv, zsend, zrecv, gsend, grecv, held, spread,
    load_sem, cs_sem, cr_sem, xs_sem, xr_sem, zs_sem, zr_sem, ss_sem, sr_sem,
    gs_sem, gr_sem, bs_sem, br_sem, as_sem, ar_sem, across_ready, near_ready, far_ready,
):
    gx, gy = lax.axis_index("gx"), lax.axis_index("gy")
    my, mzl, mc = gx // 16, (gx // 2) % 8, gx % 2
    mzh, mx = gy // 4, gy % 4
    mz = mzh * 8 + mzl

    def at(y, z, c, x):
        return (y * 16 + (z % 8) * 2 + c, (z // 8) * 4 + x)

    sibling = at(my, mz, 1 - mc, mx)
    def partner(x, y):
        return at(y % 4, mz, mc, x % 4)

    steps = (10, 6, 14, 9, 11, 5, 7, 13, 15, 2, 8, 1, 3, 4, 12)
    batch, half = mx // 2, mx % 2
    column = []
    for d in (8, 7, 9, 6, 10, 5, 11, 4, 12, 3, 13, 2, 14, 1, 15):
        z = (mz + d) % 16
        column.append((d, z, at(my, z, mc, mx)))
    row = []
    for d in (2, 1, 3):
        x = (mx + d) % 4
        row.append((d, x, at(my, mz, mc, x)))

    def signal(semaphore, peers):
        for peer in peers:
            pl.semaphore_signal(semaphore, inc=1, device_id=peer, device_id_type=MESH)

    barrier = pltpu.get_barrier_semaphore()
    across = [at((my + d) % 4, mz, mc, mx) for d in (2, 1, 3)]
    along = {d: at(my, (mz + d) % 16, mc, mx) for d in (1, 2, 4, 12, 14, 15)}
    near = [sibling] + [p[-1] for p in row] + across + [along[d] for d in (2, 14, 1, 15)]
    signal(barrier, near)

    loads = []

    def load(src, dst):
        copy = pltpu.make_async_copy(src, dst, load_sem.at[len(loads)])
        copy.start()
        loads.append(copy)
        return copy

    first_in = load(table_hbm.at[1 - mc], table.at[1 - mc])
    field_in = [load(field_hbm.at[b], field.at[b]) for b in range(2)]
    second_in = load(table_hbm.at[mc], table.at[mc])

    index = lax.broadcasted_iota(jnp.int32, (16, 128), 0)
    lane = lax.broadcasted_iota(jnp.int32, (16, 128), 1)
    kx = (lane % 4) * 4 + (index % 8) // 2
    ky = (index % 2) * 4 + jnp.where(lane < 4, 1 - mc, mc) * 2 + index // 8
    x_phase = ((kx * (gx * ROWS)) % NX).astype(F32) * (1.0 / NX)
    y_phase = ((ky * (gy * COLS)) % NY).astype(F32) * (1.0 / NY)
    phase = x_phase + y_phase
    phase = jnp.where(phase >= 1.0, phase - 1.0, phase)
    phase = jnp.where(phase >= 0.5, phase - 1.0, phase)
    cos0 = jnp.cos(phase * (2.0 * math.pi))
    sin0 = jnp.sin(phase * (2.0 * math.pi))

    def make_basis(core, column0):
        for y in range(4):
            at_lane = slice(column0 + y, column0 + y + 1)
            c0 = jnp.broadcast_to(cos0[:, at_lane], (16, 128))
            s0 = jnp.broadcast_to(sin0[:, at_lane], (16, 128))
            for t in range(4):
                lanes = pl.ds(t * 128, 128)
                cd = table[core, y, 0, :, lanes]
                sd = table[core, y, 1, :, lanes]
                re = c0 * cd - s0 * sd
                im = -(s0 * cd + c0 * sd)
                for j in range(2):
                    rows = slice(j * 8, j * 8 + 8)
                    both = jnp.concatenate([re[rows], im[rows]], axis=0)
                    basis[core, y, j, :, lanes] = both.astype(BF16)

    def forward(core, b):
        rows = basis[core].reshape(128, CELLS)
        return jnp.dot(rows, field[b], preferred_element_type=F32)

    first_in.wait()
    make_basis(1 - mc, 0)
    core_copies = []
    for b in range(2):
        field_in[b].wait()
        part = forward(1 - mc, b)
        csend[b] = part.astype(BF16)
        if b == 0:
            pl.semaphore_wait(barrier, 11)
            signal(across_ready, across)
            signal(near_ready, [along[2], along[14]])
        copy = pltpu.make_async_remote_copy(
            src_ref=csend.at[b], dst_ref=crecv.at[b], send_sem=cs_sem.at[b], recv_sem=cr_sem.at[b],
            device_id=sibling, device_id_type=MESH,
        )
        copy.start()
        core_copies.append(copy)
    weight_in = load(weight_hbm.at[half], wv.at[:, pl.ds(pl.multiple_of(mx * 64, 64), 64)])
    skip_in = load(skip_hbm, skip)
    inner_in = load(inner_hbm, inner)
    outer_in = load(outer_hbm, outer)
    second_in.wait()
    make_basis(mc, 4)
    own[0] = forward(mc, 0)

    def plane_copy(x, dx, y, dy):
        return pltpu.make_async_remote_copy(
            src_ref=xsend.at[x // 2, (y % 4) * 2 + x % 2], dst_ref=xrecv.at[dy * 4 + dx],
            send_sem=xs_sem.at[dy * 4 + dx], recv_sem=xr_sem.at[dy * 4 + dx],
            device_id=partner(x, y), device_id_type=MESH,
        )

    for b in range(2):
        if b == 1:
            own[1] = forward(mc, 1)
        core_copies[b].wait_recv()
        xsend[b] = (own[b] + crecv[b].astype(F32)).astype(BF16).reshape(8, 16, WIDTH)
        if b == 0:
            pl.semaphore_wait(across_ready, 3)
        for dy in (2, 1, 3, 0):
            for x in (2 * b, 2 * b + 1):
                dx = (x + 4 - mx) % 4
                if dy:
                    plane_copy(x, dx, my + dy, dy).start()
                else:

                    @pl.when(dx != 0)
                    def _():
                        plane_copy(x, dx, my, 0).start()

    pl.semaphore_wait(near_ready, 2)
    signal(far_ready, [along[4], along[12]])
    skip_in.wait()
    for b in range(2):
        pre[b] = jnp.dot(field[b], skip[...], preferred_element_type=F32)

    row_copies = []
    for d, x, peer in row:
        copy = pltpu.make_async_remote_copy(
            src_ref=weight_hbm.at[x % 2], dst_ref=wv.at[:, pl.ds(pl.multiple_of(mx * 64, 64), 64)],
            send_sem=ss_sem.at[d], recv_sem=sr_sem.at[d], device_id=peer, device_id_type=MESH,
        )
        row_copies.append(copy)

    mine = pl.ds(pl.multiple_of((my * 2 + half) * 16, 16), 16)
    total = own[batch, mine, :] + crecv[batch, mine, :].astype(F32)
    plane_copies = [plane_copy((mx + d) % 4, d % 4, my + d // 4, d // 4) for d in steps]
    for copy, d in reversed(list(zip(plane_copies, steps))):
        copy.wait_recv()
        total = total + xrecv[d].astype(F32)
        if d == 7:
            for weights in row_copies:
                weights.start()
    for ri in range(2):
        for t in range(4):
            zsend[pl.ds(ri * 4 + t, 8, stride=8), :] = total[ri * 8 : ri * 8 + 8, t * 128 : t * 128 + 128]

    pl.semaphore_wait(far_ready, 2)
    column_copies = []
    for d, z, peer in column:
        copy = pltpu.make_async_remote_copy(
            src_ref=zsend.at[pl.ds(pl.multiple_of((z % 8) * 8, 8), 8)], dst_ref=zrecv.at[d],
            send_sem=zs_sem.at[d], recv_sem=zr_sem.at[d], device_id=peer, device_id_type=MESH,
        )
        copy.start()
        column_copies.append(copy)

    for t in range(4):
        cells = pl.ds(t * 128, 128)
        basis_t[cells, :] = basis[:, :, :, :, cells].reshape(256, 128).T
    inner_in.wait()
    for t in range(8):
        units = pl.ds(t * 128, 128)
        inner_t[:, units] = inner[units, :].T
    for copy in core_copies + plane_copies:
        copy.wait_send()

    total = zsend[pl.ds(pl.multiple_of(mzl * 8, 8), 8), :]
    for copy, (d, _, _) in reversed(list(zip(column_copies, column))):
        copy.wait_recv()
        total = total + zrecv[d]
    spectrum = (total * SPECTRUM_SCALE).astype(BF16).astype(F32)

    weight_in.wait()
    for copy in row_copies:
        copy.wait_recv()
    parts = [
        jnp.concatenate([spectrum[ri * 4 + t : ri * 4 + t + 1] for t in range(4)], axis=1)
        for ri in range(2)
    ]
    modes = jnp.concatenate(parts * 4, axis=0).astype(BF16)
    nt = (((1,), (1,)), ((), ()))
    by_re = lax.dot_general(modes, wv[0], nt, preferred_element_type=F32)
    by_im = lax.dot_general(modes, wv[1], nt, preferred_element_type=F32)
    mixed_re = by_re[0:1] - by_im[1:2]
    mixed_im = by_im[0:1] + by_re[1:2]
    mixed = [v[:, t * 128 : t * 128 + 128] for v in (mixed_re, mixed_im) for t in range(2)]
    mixed = jnp.concatenate(mixed + mixed, axis=0).astype(BF16).astype(F32)

    gsend[...] = mixed
    back_copies = []
    for d, z, peer in column:
        copy = pltpu.make_async_remote_copy(
            src_ref=gsend, dst_ref=grecv.at[pl.ds(pl.multiple_of(mz * 8, 8), 8)],
            send_sem=gs_sem.at[d], recv_sem=gr_sem.at[d], device_id=peer, device_id_type=MESH,
        )
        copy.start()
        back_copies.append(copy)
    grecv[pl.ds(pl.multiple_of(mz * 8, 8), 8), :] = mixed
    outer_in.wait()
    for copy in column_copies + row_copies:
        copy.wait_send()
    for copy in reversed(back_copies):
        copy.wait_recv()

    for ri in range(2):
        for h in range(2):
            for t in range(2):
                part = grecv[pl.ds(h * 64 + ri * 2 + t, 8, stride=8), :]
                held[ri * 8 : ri * 8 + 8, pl.ds(h * 256 + t * 128, 128)] = part
    spread[mc, my, batch, half] = held[...].astype(BF16)

    block = spread.at[mc, my, batch, half]

    def arrival(d):
        return pltpu.make_async_remote_copy(
            src_ref=block, dst_ref=block, send_sem=bs_sem.at[d], recv_sem=br_sem.at[d],
            device_id=partner(mx + d % 4, my + d // 4), device_id_type=MESH,
        )

    for d in steps:
        arrival(d).start()
    for copy in back_copies:
        copy.wait_send()

    pair_copies = [[], []]

    def pass_on(dy, b):
        y = (my + 4 - dy) % 4
        for x in (2 * b, 2 * b + 1):
            d = dy * 4 + (mx + 4 - x) % 4
            if dy:
                arrival(d).wait_recv()
            else:

                @pl.when(x != mx)
                def _():
                    arrival(d).wait_recv()

        copy = pltpu.make_async_remote_copy(
            src_ref=spread.at[mc, y, b], dst_ref=spread.at[mc, y, b],
            send_sem=as_sem.at[dy, b], recv_sem=ar_sem.at[dy, b],
            device_id=sibling, device_id_type=MESH,
        )
        copy.start()
        pair_copies[b].append(copy)

    def finish(b):
        modes = spread[:, :, b].reshape(256, WIDTH)
        spectral = jnp.dot(basis_t[...], modes, preferred_element_type=F32)
        active = gelu(spectral * FIELD_SCALE + pre[b]).astype(BF16)
        hidden = jnp.dot(active, inner_t[...], preferred_element_type=F32)
        hidden = gelu(hidden).astype(BF16)
        added = jnp.dot(hidden, outer[...], preferred_element_type=F32)
        out_ref[b] = (active.astype(F32) + added).astype(BF16)

    for dy in (0, 1, 3, 2):
        pass_on(dy, 0)
        pass_on(dy, 1)
    for copy in pair_copies[0]:
        copy.wait_recv()
    finish(0)
    for d in steps:
        arrival(d).wait_send()
    for copy in pair_copies[0] + pair_copies[1]:
        copy.wait_send()
    for copy in pair_copies[1]:
        copy.wait_recv()
    finish(1)


def local(grid_field, spectral_weight, skip_weight, inner_weight, outer_weight):
    table = jnp.asarray(local_tables())
    field = grid_field.reshape(2, CELLS, WIDTH)
    weight = jnp.swapaxes(spectral_weight, 2, 3)
    dma = pltpu.SemaphoreType.DMA
    operands = (field, weight, skip_weight, inner_weight, outer_weight, table)
    operands = [pltpu.with_memory_space_constraint(v, pltpu.HBM) for v in operands]
    out = pl.pallas_call(
        body,
        out_shape=jax.ShapeDtypeStruct((2, CELLS, WIDTH), BF16),
        in_specs=[pl.BlockSpec(memory_space=pltpu.HBM)] * 6,
        out_specs=pl.BlockSpec(memory_space=pltpu.VMEM),
        scratch_shapes=[
            pltpu.VMEM((2, CELLS, WIDTH), BF16),
            pltpu.VMEM((2, 256, WIDTH), BF16),
            pltpu.VMEM((WIDTH, WIDTH), BF16),
            pltpu.VMEM((HIDDEN, WIDTH), BF16),
            pltpu.VMEM((HIDDEN, WIDTH), BF16),
            pltpu.VMEM((2, 4, 2, 16, CELLS), F32),
            pltpu.VMEM((2, 4, 2, 16, CELLS), BF16),
            pltpu.VMEM((CELLS, 256), BF16),
            pltpu.VMEM((WIDTH, HIDDEN), BF16),
            pltpu.VMEM((2, CELLS, WIDTH), F32),
            pltpu.VMEM((2, 128, WIDTH), BF16),
            pltpu.VMEM((2, 128, WIDTH), BF16),
            pltpu.VMEM((2, 128, WIDTH), F32),
            pltpu.VMEM((2, 8, 16, WIDTH), BF16),
            pltpu.VMEM((16, 16, WIDTH), BF16),
            pltpu.VMEM((64, 128), F32),
            pltpu.VMEM((16, 8, 128), F32),
            pltpu.VMEM((8, 128), F32),
            pltpu.VMEM((128, 128), F32),
            pltpu.VMEM((16, WIDTH), F32),
            pltpu.VMEM((2, 4, 2, 2, 16, WIDTH), BF16),
            dma((12,)),
            dma((2,)), dma((2,)),
            dma((16,)), dma((16,)),
            dma((16,)), dma((16,)),
            dma((4,)), dma((4,)),
            dma((16,)), dma((16,)),
            dma((16,)), dma((16,)),
            dma((4, 2)), dma((4, 2)),
            pltpu.SemaphoreType.REGULAR, pltpu.SemaphoreType.REGULAR, pltpu.SemaphoreType.REGULAR,
        ],
        compiler_params=pltpu.CompilerParams(
            collective_id=0, has_side_effects=True, vmem_limit_bytes=40 << 20
        ),
        cost_estimate=pl.CostEstimate(flops=3_400_000_000, bytes_accessed=7 << 20, transcendentals=1_600_000),
    )(*operands)
    return out.reshape(grid_field.shape)


def solution(mesh):
    in_specs = (P(None, "gx", "gy", None), P("gx", None, None, "gy"), P(), P(), P())
    out_specs = P(None, "gx", "gy", None)
    return jax.shard_map(local, mesh=mesh, in_specs=in_specs, out_specs=out_specs, check_vma=False)
```
